32 devices in a mesh: grp: 2 (over y), row: 8 (over z, x), sub: 2 (over core).
Axes of the slice: x: 2, y: 2, z: 4, core: 2. Of those that a mesh axis runs over, the one named last changes fastest.
Arguments:
- pair_rep: bfloat16 [64, 32, 128], P(('grp', 'row'), 'sub'), parts along dimension 0, may hold values from -6 to 6
- norm_gain: float32 [128], replicated, may hold values from 0.1 to 1.9
- norm_bias: float32 [128], replicated, may hold values from -3 to 3
- w_a_proj: bfloat16 [128, 128], replicated, may hold values from -0.5 to 0.5
- w_a_gate: bfloat16 [128, 128], replicated, may hold values from -0.5 to 0.5
- w_b_proj: bfloat16 [128, 128], replicated, may hold values from -0.5 to 0.5
- w_b_gate: bfloat16 [128, 128], replicated, may hold values from -0.5 to 0.5
- w_gate: bfloat16 [128, 128], replicated, may hold values from -0.5 to 0.5
- out_gain: float32 [128], replicated, may hold values from 0.1 to 1.9
- out_bias: float32 [128], replicated, may hold values from -3 to 3
- w_out: bfloat16 [128, 128], replicated, may hold values from -0.5 to 0.5
Outputs:
- update: bfloat16 [64, 32, 128], P(('grp', 'row'), 'sub'), parts along dimension 0
The draws below stay inside these ranges and needn't reach their ends.
There are 2 independent parts, one for each index of `grp`. The reference program is written for one: setup_inputs(seed, part) draws one part's arguments, and reference() takes and returns one part's arrays. A program takes and returns all parts, laid end to end along the dimension named above; an argument that names none is the same for every part. Nothing has to cross between parts.
All inputs are finite; a program needn't handle non-finite values.
Results may differ from the reference program's by a relative error of at most 0.012.
Values may be sent and summed in bfloat16 or wider, within the bound.
A program may use at most 64 MiB of HBM per device.

```python
import jax
import jax.numpy as jnp
from jax import lax

C = 128
H = 128
ROWS_DEV = 4
TOKENS = 32
N_ROW = 8


def block_levels(stream_key, dims, pieces, least, high):
    def one(position, blocks):
        heights = jax.random.uniform(jax.random.fold_in(jax.random.fold_in(stream_key, 6), position), (blocks,), jnp.float32, least / len(pieces), high / len(pieces))
        return jnp.repeat(jnp.exp(heights), dims[position] // blocks).reshape((-1,) + (1,) * (len(dims) - position - 1))

    level = one(*pieces[0])
    for cut in pieces[1:]:
        level = level * one(*cut)
    return level


def bell_draw(rng, shape, deviation, most, split=(), dtype=jnp.bfloat16):
    level = block_levels(rng, shape, split, -0.22, 0.18) if split else 1.0
    entries = jax.random.normal(rng, shape, jnp.float32) * deviation * level
    return jnp.minimum(jnp.maximum(entries, -most), most).astype(dtype)


def setup_inputs(seed: int = 0, part: int = 0) -> dict:
    key_list = jax.random.split(jax.random.key(seed), 12)
    part_keys = jax.random.split(jax.random.fold_in(key_list[11], part), 12)
    pair_rep = bell_draw(part_keys[0], (TOKENS, TOKENS, C), 1.0, 6.0, ((0, 8), (1, 2)))
    norm_gain = jnp.clip(1.0 + 0.18 * jax.random.normal(key_list[1], (C,), jnp.float32), 0.1, 1.9)
    norm_bias = bell_draw(key_list[2], (C,), 0.5, 3.0, (), jnp.float32)
    w_a_proj = bell_draw(key_list[3], (C, H), C ** -0.5, 0.5)
    w_a_gate = bell_draw(key_list[4], (C, H), C ** -0.5, 0.5)
    w_b_proj = bell_draw(key_list[5], (C, H), C ** -0.5, 0.5)
    w_b_gate = bell_draw(key_list[6], (C, H), C ** -0.5, 0.5)
    w_gate = bell_draw(key_list[7], (C, C), C ** -0.5, 0.5)
    out_gain = jnp.clip(1.0 + 0.18 * jax.random.normal(key_list[8], (H,), jnp.float32), 0.1, 1.9)
    out_bias = bell_draw(key_list[9], (H,), 0.5, 3.0, (), jnp.float32)
    w_out = bell_draw(key_list[10], (H, C), H ** -0.5, 0.5)
    return dict(pair_rep=pair_rep, norm_gain=norm_gain, norm_bias=norm_bias, w_a_proj=w_a_proj, w_a_gate=w_a_gate, w_b_proj=w_b_proj, w_b_gate=w_b_gate, w_gate=w_gate, out_gain=out_gain, out_bias=out_bias, w_out=w_out)


EPSILON = 1e-05

def layer_norm(values, gain, shift, axis):
    centred = values - lax.optimization_barrier(jnp.mean(values, axis=axis, keepdims=True))
    variance = lax.optimization_barrier(jnp.mean(centred * centred, axis=axis, keepdims=True))
    return centred * lax.rsqrt(variance + EPSILON) * gain + shift

def reference(pair_rep, norm_gain, norm_bias, w_a_proj, w_a_gate, w_b_proj, w_b_gate, w_gate, out_gain, out_bias, w_out):
    w_inner = jnp.concatenate([w_a_proj, w_a_gate, w_b_proj, w_b_gate], axis=1)

    def project(block):
        normed = layer_norm(block.astype(jnp.float32), norm_gain, norm_bias, -1).astype(jnp.bfloat16)
        flat_rows = normed.reshape(-1, C)
        inner = jnp.dot(flat_rows, w_inner, preferred_element_type=jnp.float32)
        left_act = (jax.nn.sigmoid(inner[:, H:2 * H]) * inner[:, :H]).astype(jnp.bfloat16)
        right_act = (jax.nn.sigmoid(inner[:, 3 * H:4 * H]) * inner[:, 2 * H:3 * H]).astype(jnp.bfloat16)
        gating = jax.nn.sigmoid(jnp.dot(flat_rows, w_gate, preferred_element_type=jnp.float32)).astype(jnp.bfloat16)
        return (left_act.reshape(ROWS_DEV, TOKENS, H), right_act.reshape(ROWS_DEV, TOKENS, H), gating.reshape(ROWS_DEV, TOKENS, C))
    blocks = pair_rep.reshape(N_ROW, ROWS_DEV, TOKENS, C)
    left_act, right_act, gating = lax.map(project, blocks)
    left_t = jnp.transpose(left_act.reshape(TOKENS, TOKENS, H), (2, 0, 1))
    right_t = jnp.transpose(right_act.reshape(TOKENS, TOKENS, H), (2, 0, 1))

    def channel(operands):
        left_one, right_one = operands
        return jnp.dot(left_one, right_one.T, preferred_element_type=jnp.float32).astype(jnp.bfloat16)
    triangle = lax.map(channel, (left_t, right_t))
    tri_rows = jnp.transpose(triangle, (1, 2, 0)).reshape(N_ROW, ROWS_DEV, TOKENS, H)

    def finish(operands):
        tri_block, gate_block = operands
        normed = layer_norm(tri_block.astype(jnp.float32), out_gain, out_bias, -1).astype(jnp.bfloat16)
        mixed = jnp.dot(normed.reshape(-1, H), w_out, preferred_element_type=jnp.float32)
        result = gate_block.reshape(-1, C).astype(jnp.float32) * mixed
        return result.astype(jnp.bfloat16).reshape(ROWS_DEV, TOKENS, C)
    return lax.map(finish, (tri_rows, gating)).reshape(TOKENS, TOKENS, C)
```

```python
import functools

import jax
import jax.numpy as jnp
from jax import lax
from jax.experimental import pallas as pl
from jax.experimental.pallas import tpu as pltpu
from jax.sharding import PartitionSpec as P

EPSILON = 1e-05


def layer_norm(values, gain, shift, axis):
    centred = values - jnp.mean(values, axis=axis, keepdims=True)
    variance = jnp.mean(centred * centred, axis=axis, keepdims=True)
    return centred * lax.rsqrt(variance + EPSILON) * gain + shift


def per_device(
    pair_rep,
    norm_gain,
    norm_bias,
    w_a_proj,
    w_a_gate,
    w_b_proj,
    w_b_gate,
    w_gate,
    out_gain,
    out_bias,
    w_out,
):
    hidden = w_a_proj.shape[1]
    w_inner = jnp.concatenate([w_a_proj, w_a_gate, w_b_proj, w_b_gate], axis=1)
    normed = layer_norm(pair_rep.astype(jnp.float32), norm_gain, norm_bias, -1).astype(jnp.bfloat16)
    inner = jnp.einsum("rkc,cm->mrk", normed, w_inner, preferred_element_type=jnp.float32)
    left_local = (jax.nn.sigmoid(inner[hidden : 2 * hidden]) * inner[:hidden]).astype(jnp.bfloat16)
    right_local = (
        jax.nn.sigmoid(inner[3 * hidden : 4 * hidden]) * inner[2 * hidden : 3 * hidden]
    ).astype(jnp.bfloat16)
    gating = jax.nn.sigmoid(
        jnp.einsum("rkc,cd->rkd", normed, w_gate, preferred_element_type=jnp.float32)
    ).astype(jnp.bfloat16)
    left_chan, right_chan = (
        lax.all_to_all(left_local, "row", split_axis=0, concat_axis=1, tiled=True),
        lax.all_to_all(right_local, "row", split_axis=0, concat_axis=1, tiled=True),
    )
    left_rows = lax.all_to_all(left_chan, "sub", split_axis=1, concat_axis=2, tiled=True)
    triangle = jnp.einsum(
        "hik,hjk->hij",
        left_rows,
        lax.all_gather(right_chan, "sub", axis=2, tiled=True),
        preferred_element_type=jnp.float32,
    ).astype(jnp.bfloat16)
    regrouped = lax.all_to_all(
        lax.all_to_all(triangle, "sub", split_axis=2, concat_axis=1, tiled=True),
        "row",
        split_axis=1,
        concat_axis=0,
        tiled=True,
    )
    hidden_normed = layer_norm(
        regrouped.astype(jnp.float32), out_gain[:, None, None], out_bias[:, None, None], 0
    ).astype(jnp.bfloat16)
    mixed = jnp.einsum("hrj,hc->rjc", hidden_normed, w_out, preferred_element_type=jnp.float32)
    return (gating.astype(jnp.float32) * mixed).astype(jnp.bfloat16)


def kernel(
    n_row,
    pair_hbm,
    ngain_hbm,
    nbias_hbm,
    wap_hbm,
    wag_hbm,
    wbp_hbm,
    wbg_hbm,
    wg_hbm,
    ogain_hbm,
    obias_hbm,
    wo_hbm,
    out_ref,
    pair_v,
    vec_v,
    w_v,
    wo_v,
    right_send,
    right_buf,
    left_buf,
    tri_v,
    in_sem,
    send_sem,
    recv_sem,
    left_sem,
):
    rows, cols, chan = pair_v.shape
    hidden = right_send.shape[-1]
    half = n_row // 2
    row = lax.axis_index("row")
    sub = lax.axis_index("sub")
    other = 1 - sub
    owner = row // half
    slot = lax.rem(row, half)

    loads = [
        pltpu.make_async_copy(pair_hbm, pair_v, in_sem.at[0]),
        pltpu.make_async_copy(ngain_hbm, vec_v.at[0], in_sem.at[1]),
        pltpu.make_async_copy(nbias_hbm, vec_v.at[1], in_sem.at[2]),
        pltpu.make_async_copy(wbp_hbm, w_v.at[:, 0:hidden], in_sem.at[3]),
        pltpu.make_async_copy(wbg_hbm, w_v.at[:, hidden : 2 * hidden], in_sem.at[4]),
        pltpu.make_async_copy(wap_hbm, w_v.at[:, 2 * hidden : 3 * hidden], in_sem.at[5]),
        pltpu.make_async_copy(wag_hbm, w_v.at[:, 3 * hidden : 4 * hidden], in_sem.at[6]),
        pltpu.make_async_copy(wg_hbm, w_v.at[:, 4 * hidden : 4 * hidden + chan], in_sem.at[7]),
        pltpu.make_async_copy(ogain_hbm, vec_v.at[2], in_sem.at[8]),
        pltpu.make_async_copy(obias_hbm, vec_v.at[3], in_sem.at[9]),
        pltpu.make_async_copy(wo_hbm, wo_v, in_sem.at[10]),
    ]
    for load in loads:
        load.start()

    barrier = pltpu.get_barrier_semaphore()
    for step in range(half):
        for source_sub in range(2):
            source = sub * half + step
            mine = jnp.logical_and(source == row, sub == source_sub)

            @pl.when(jnp.logical_not(mine))
            def _():
                pl.semaphore_signal(
                    barrier,
                    inc=1,
                    device_id={"row": source, "sub": source_sub},
                    device_id_type=pl.DeviceIdType.MESH,
                )

    @pl.when(owner != sub)
    def _():
        pl.semaphore_signal(
            barrier, inc=1, device_id={"sub": other}, device_id_type=pl.DeviceIdType.MESH
        )

    for load in loads[:3]:
        load.wait()
    pair = pair_v[...].astype(jnp.float32).reshape(rows * cols, chan)
    normed = layer_norm(pair, vec_v[0], vec_v[1], -1).astype(jnp.bfloat16)
    for load in loads[3:5]:
        load.wait()
    inner = jnp.dot(normed, w_v[:, 0 : 2 * hidden], preferred_element_type=jnp.float32)
    right = jax.nn.sigmoid(inner[:, hidden:]) * inner[:, :hidden]
    right = right.astype(jnp.bfloat16).reshape(rows, cols, hidden)
    right_send[...] = right

    @pl.when(owner == sub)
    def _():
        right_buf[slot, sub] = right

    for load in loads[5:7]:
        load.wait()
    inner = jnp.dot(
        normed, w_v[:, 2 * hidden : 4 * hidden], preferred_element_type=jnp.float32
    )
    left = jax.nn.sigmoid(inner[:, hidden:]) * inner[:, :hidden]
    left_buf[sub] = left.astype(jnp.bfloat16).reshape(rows, cols, hidden)

    pl.semaphore_wait(barrier, n_row)

    left_copy = pltpu.make_async_remote_copy(
        src_ref=left_buf.at[sub],
        dst_ref=left_buf.at[sub],
        send_sem=send_sem.at[n_row],
        recv_sem=left_sem,
        device_id={"sub": other},
        device_id_type=pl.DeviceIdType.MESH,
    )
    copies = []
    for step in range(n_row):
        target = lax.rem(row + step, n_row)
        copies.append(
            pltpu.make_async_remote_copy(
                src_ref=right_send,
                dst_ref=right_buf.at[slot, sub],
                send_sem=send_sem.at[step],
                recv_sem=recv_sem.at[slot, sub],
                device_id={"row": target, "sub": owner},
                device_id_type=pl.DeviceIdType.MESH,
            )
        )
    for step in range(1, n_row):
        copies[step].start()
    left_copy.start()

    @pl.when(owner != sub)
    def _():
        copies[0].start()

    loads[7].wait()
    gating = jax.nn.sigmoid(
        jnp.dot(
            normed, w_v[:, 4 * hidden : 4 * hidden + chan], preferred_element_type=jnp.float32
        )
    ).astype(jnp.bfloat16)
    for load in loads[8:]:
        load.wait()

    left_copy.wait_recv()
    left_all = left_buf[...].astype(jnp.float32)
    for source in range(half):
        for source_sub in range(2):
            mine = jnp.logical_and(sub * half + source == row, sub == source_sub)

            @pl.when(jnp.logical_not(mine))
            def _():
                pltpu.make_async_remote_copy(
                    src_ref=right_send,
                    dst_ref=right_buf.at[source, source_sub],
                    send_sem=send_sem.at[0],
                    recv_sem=recv_sem.at[source, source_sub],
                    device_id={"sub": other},
                    device_id_type=pl.DeviceIdType.MESH,
                ).wait_recv()

        block = right_buf[source].astype(jnp.float32)
        for i in range(rows):
            prod = left_all[:, i][:, None] * block
            prod = prod[0] + prod[1]
            prod = jnp.sum(prod.reshape(rows, cols // 8, 8, hidden), axis=1)
            tri_v[i, source * rows : (source + 1) * rows, :] = jnp.sum(prod, axis=1)

    tri = tri_v[...].reshape(rows * cols, hidden).astype(jnp.bfloat16).astype(jnp.float32)
    hidden_normed = layer_norm(tri, vec_v[2], vec_v[3], -1).astype(jnp.bfloat16)
    mixed = jnp.dot(hidden_normed, wo_v[...], preferred_element_type=jnp.float32)
    out = (gating.astype(jnp.float32) * mixed).astype(jnp.bfloat16)
    out_ref[...] = out.reshape(rows, cols, chan)

    left_copy.wait_send()
    for step in range(1, n_row):
        copies[step].wait_send()

    @pl.when(owner != sub)
    def _():
        copies[0].wait_send()


def one_round(n_row, pair_rep, norm_gain, norm_bias, *rest):
    w_a_proj, w_a_gate, w_b_proj, w_b_gate, w_gate, out_gain, out_bias, w_out = rest
    rows, cols, chan = pair_rep.shape
    hidden = w_a_proj.shape[1]
    half = n_row // 2
    hbm = pl.BlockSpec(memory_space=pltpu.HBM)
    return pl.pallas_call(
        functools.partial(kernel, n_row),
        out_shape=jax.ShapeDtypeStruct((rows, cols, chan), jnp.bfloat16),
        in_specs=[hbm] * 11,
        out_specs=pl.BlockSpec(memory_space=pltpu.VMEM),
        scratch_shapes=[
            pltpu.VMEM((rows, cols, chan), jnp.bfloat16),
            pltpu.VMEM((4, 1, chan), jnp.float32),
            pltpu.VMEM((chan, 4 * hidden + chan), jnp.bfloat16),
            pltpu.VMEM((hidden, chan), jnp.bfloat16),
            pltpu.VMEM((rows, cols, hidden), jnp.bfloat16),
            pltpu.VMEM((half, 2, rows, cols, hidden), jnp.bfloat16),
            pltpu.VMEM((2, rows, cols, hidden), jnp.bfloat16),
            pltpu.VMEM((rows, cols, hidden), jnp.float32),
            pltpu.SemaphoreType.DMA((11,)),
            pltpu.SemaphoreType.DMA((n_row + 1,)),
            pltpu.SemaphoreType.DMA((half, 2)),
            pltpu.SemaphoreType.DMA,
        ],
        compiler_params=pltpu.CompilerParams(
            collective_id=0, has_side_effects=True, vmem_limit_bytes=16 * 2**20
        ),
    )(
        pair_rep,
        norm_gain.reshape(1, chan),
        norm_bias.reshape(1, chan),
        w_a_proj,
        w_a_gate,
        w_b_proj,
        w_b_gate,
        w_gate,
        out_gain.reshape(1, hidden),
        out_bias.reshape(1, hidden),
        w_out,
    )


def body(n_row, n_sub, *operands):
    rows, cols, _ = operands[0].shape
    hidden = operands[3].shape[1]
    gathered = cols * cols * n_sub * hidden * 2
    if n_sub == 2 and n_row % 2 == 0 and cols % 16 == 0 and gathered <= 4 * 2**20:
        return one_round(n_row, *operands)
    return per_device(*operands)


def solution(mesh):
    in_specs = (P(("grp", "row"), "sub", None), P(), P(), P(), P(), P(), P(), P(), P(), P(), P())
    out_specs = P(("grp", "row"), "sub", None)
    return jax.shard_map(
        functools.partial(body, mesh.shape["row"], mesh.shape["sub"]),
        mesh=mesh,
        in_specs=in_specs,
        out_specs=out_specs,
        check_vma=False,
    )
```

```python
import functools

import jax
import jax.numpy as jnp
from jax import lax
from jax.experimental import pallas as pl
from jax.experimental.pallas import tpu as pltpu
from jax.sharding import PartitionSpec as P

EPSILON = 1e-05


def layer_norm(values, gain, shift, axis):
    centred = values - jnp.mean(values, axis=axis, keepdims=True)
    variance = jnp.mean(centred * centred, axis=axis, keepdims=True)
    return centred * lax.rsqrt(variance + EPSILON) * gain + shift


def per_device(
    pair_rep,
    norm_gain,
    norm_bias,
    w_a_proj,
    w_a_gate,
    w_b_proj,
    w_b_gate,
    w_gate,
    out_gain,
    out_bias,
    w_out,
):
    hidden = w_a_proj.shape[1]
    w_inner = jnp.concatenate([w_a_proj, w_a_gate, w_b_proj, w_b_gate], axis=1)
    normed = layer_norm(pair_rep.astype(jnp.float32), norm_gain, norm_bias, -1).astype(jnp.bfloat16)
    inner = jnp.einsum("rkc,cm->mrk", normed, w_inner, preferred_element_type=jnp.float32)
    left_local = (jax.nn.sigmoid(inner[hidden : 2 * hidden]) * inner[:hidden]).astype(jnp.bfloat16)
    right_local = (
        jax.nn.sigmoid(inner[3 * hidden : 4 * hidden]) * inner[2 * hidden : 3 * hidden]
    ).astype(jnp.bfloat16)
    gating = jax.nn.sigmoid(
        jnp.einsum("rkc,cd->rkd", normed, w_gate, preferred_element_type=jnp.float32)
    ).astype(jnp.bfloat16)
    left_chan, right_chan = (
        lax.all_to_all(left_local, "row", split_axis=0, concat_axis=1, tiled=True),
        lax.all_to_all(right_local, "row", split_axis=0, concat_axis=1, tiled=True),
    )
    left_rows = lax.all_to_all(left_chan, "sub", split_axis=1, concat_axis=2, tiled=True)
    triangle = jnp.einsum(
        "hik,hjk->hij",
        left_rows,
        lax.all_gather(right_chan, "sub", axis=2, tiled=True),
        preferred_element_type=jnp.float32,
    ).astype(jnp.bfloat16)
    regrouped = lax.all_to_all(
        lax.all_to_all(triangle, "sub", split_axis=2, concat_axis=1, tiled=True),
        "row",
        split_axis=1,
        concat_axis=0,
        tiled=True,
    )
    hidden_normed = layer_norm(
        regrouped.astype(jnp.float32), out_gain[:, None, None], out_bias[:, None, None], 0
    ).astype(jnp.bfloat16)
    mixed = jnp.einsum("hrj,hc->rjc", hidden_normed, w_out, preferred_element_type=jnp.float32)
    return (gating.astype(jnp.float32) * mixed).astype(jnp.bfloat16)


def kernel(
    n_row,
    pair_hbm,
    ngain_hbm,
    nbias_hbm,
    wap_hbm,
    wag_hbm,
    wbp_hbm,
    wbg_hbm,
    wg_hbm,
    ogain_hbm,
    obias_hbm,
    wo_hbm,
    out_ref,
    pair_v,
    vec_v,
    w_v,
    wo_v,
    right_send,
    right_buf,
    left_buf,
    tri_v,
    in_sem,
    send_sem,
    recv_sem,
    left_sem,
):
    rows, cols, chan = pair_v.shape
    hidden = right_send.shape[-1]
    half = n_row // 2
    row = lax.axis_index("row")
    sub = lax.axis_index("sub")
    other = 1 - sub
    owner = row // half
    slot = lax.rem(row, half)

    loads = [
        pltpu.make_async_copy(pair_hbm, pair_v, in_sem.at[0]),
        pltpu.make_async_copy(ngain_hbm, vec_v.at[0], in_sem.at[1]),
        pltpu.make_async_copy(nbias_hbm, vec_v.at[1], in_sem.at[2]),
        pltpu.make_async_copy(wbp_hbm, w_v.at[:, 0:hidden], in_sem.at[3]),
        pltpu.make_async_copy(wbg_hbm, w_v.at[:, hidden : 2 * hidden], in_sem.at[4]),
        pltpu.make_async_copy(wap_hbm, w_v.at[:, 2 * hidden : 3 * hidden], in_sem.at[5]),
        pltpu.make_async_copy(wag_hbm, w_v.at[:, 3 * hidden : 4 * hidden], in_sem.at[6]),
        pltpu.make_async_copy(wg_hbm, w_v.at[:, 4 * hidden : 4 * hidden + chan], in_sem.at[7]),
        pltpu.make_async_copy(ogain_hbm, vec_v.at[2], in_sem.at[8]),
        pltpu.make_async_copy(obias_hbm, vec_v.at[3], in_sem.at[9]),
        pltpu.make_async_copy(wo_hbm, wo_v, in_sem.at[10]),
    ]
    for load in loads:
        load.start()

    barrier = pltpu.get_barrier_semaphore()
    for step in range(half):
        for source_sub in range(2):
            source = sub * half + step
            mine = jnp.logical_and(source == row, sub == source_sub)

            @pl.when(jnp.logical_not(mine))
            def _():
                pl.semaphore_signal(
                    barrier,
                    inc=1,
                    device_id={"row": source, "sub": source_sub},
                    device_id_type=pl.DeviceIdType.MESH,
                )

    @pl.when(owner != sub)
    def _():
        pl.semaphore_signal(
            barrier, inc=1, device_id={"sub": other}, device_id_type=pl.DeviceIdType.MESH
        )

    for load in loads[:3]:
        load.wait()
    pair = pair_v[...].astype(jnp.float32).reshape(rows * cols, chan)
    normed = layer_norm(pair, vec_v[0], vec_v[1], -1).astype(jnp.bfloat16)
    for load in loads[3:5]:
        load.wait()
    inner = jnp.dot(normed, w_v[:, 0 : 2 * hidden], preferred_element_type=jnp.float32)
    right = jax.nn.sigmoid(inner[:, hidden:]) * inner[:, :hidden]
    right = right.astype(jnp.bfloat16).reshape(rows, cols, hidden)
    right_send[...] = right

    @pl.when(owner == sub)
    def _():
        right_buf[slot, sub] = right

    for load in loads[5:7]:
        load.wait()
    inner = jnp.dot(
        normed, w_v[:, 2 * hidden : 4 * hidden], preferred_element_type=jnp.float32
    )
    left = jax.nn.sigmoid(inner[:, hidden:]) * inner[:, :hidden]
    left_buf[sub] = left.astype(jnp.bfloat16).reshape(rows, cols, hidden)

    pl.semaphore_wait(barrier, n_row)

    left_copy = pltpu.make_async_remote_copy(
        src_ref=left_buf.at[sub],
        dst_ref=left_buf.at[sub],
        send_sem=send_sem.at[n_row],
        recv_sem=left_sem,
        device_id={"sub": other},
        device_id_type=pl.DeviceIdType.MESH,
    )
    copies = []
    for step in range(n_row):
        target = lax.rem(row + step, n_row)
        copies.append(
            pltpu.make_async_remote_copy(
                src_ref=right_send,
                dst_ref=right_buf.at[slot, sub],
                send_sem=send_sem.at[step],
                recv_sem=recv_sem.at[slot, sub],
                device_id={"row": target, "sub": owner},
                device_id_type=pl.DeviceIdType.MESH,
            )
        )
    for step in range(1, n_row):
        copies[step].start()
    left_copy.start()

    @pl.when(owner != sub)
    def _():
        copies[0].start()

    loads[7].wait()
    gating = jax.nn.sigmoid(
        jnp.dot(
            normed, w_v[:, 4 * hidden : 4 * hidden + chan], preferred_element_type=jnp.float32
        )
    ).astype(jnp.bfloat16)
    for load in loads[8:]:
        load.wait()

    left_copy.wait_recv()
    left_all = left_buf[...].astype(jnp.float32)
    for source in range(half):
        for source_sub in range(2):
            mine = jnp.logical_and(sub * half + source == row, sub == source_sub)

            @pl.when(jnp.logical_not(mine))
            def _():
                pltpu.make_async_remote_copy(
                    src_ref=right_send,
                    dst_ref=right_buf.at[source, source_sub],
                    send_sem=send_sem.at[0],
                    recv_sem=recv_sem.at[source, source_sub],
                    device_id={"sub": other},
                    device_id_type=pl.DeviceIdType.MESH,
                ).wait_recv()

        block = right_buf[source].astype(jnp.float32)
        for i in range(rows):
            prod = left_all[:, i][:, None] * block
            prod = prod[0] + prod[1]
            prod = jnp.sum(prod.reshape(rows, cols // 8, 8, hidden), axis=1)
            tri_v[i, source * rows : (source + 1) * rows, :] = jnp.sum(prod, axis=1)

    tri = tri_v[...].reshape(rows * cols, hidden).astype(jnp.bfloat16).astype(jnp.float32)
    hidden_normed = layer_norm(tri, vec_v[2], vec_v[3], -1).astype(jnp.bfloat16)
    mixed = jnp.dot(hidden_normed, wo_v[...], preferred_element_type=jnp.float32)
    out = (gating.astype(jnp.float32) * mixed).astype(jnp.bfloat16)
    out_ref[...] = out.reshape(rows, cols, chan)

    left_copy.wait_send()
    for step in range(1, n_row):
        copies[step].wait_send()

    @pl.when(owner != sub)
    def _():
        copies[0].wait_send()


def one_round(n_row, pair_rep, norm_gain, norm_bias, *rest):
    w_a_proj, w_a_gate, w_b_proj, w_b_gate, w_gate, out_gain, out_bias, w_out = rest
    rows, cols, chan = pair_rep.shape
    hidden = w_a_proj.shape[1]
    half = n_row // 2
    hbm = pl.BlockSpec(memory_space=pltpu.HBM)
    return pl.pallas_call(
        functools.partial(kernel, n_row),
        out_shape=pltpu.VMEM((rows, cols, chan), jnp.bfloat16),
        in_specs=[hbm] * 11,
        out_specs=pl.BlockSpec(memory_space=pltpu.VMEM),
        scratch_shapes=[
            pltpu.VMEM((rows, cols, chan), jnp.bfloat16),
            pltpu.VMEM((4, 1, chan), jnp.float32),
            pltpu.VMEM((chan, 4 * hidden + chan), jnp.bfloat16),
            pltpu.VMEM((hidden, chan), jnp.bfloat16),
            pltpu.VMEM((rows, cols, hidden), jnp.bfloat16),
            pltpu.VMEM((half, 2, rows, cols, hidden), jnp.bfloat16),
            pltpu.VMEM((2, rows, cols, hidden), jnp.bfloat16),
            pltpu.VMEM((rows, cols, hidden), jnp.float32),
            pltpu.SemaphoreType.DMA((11,)),
            pltpu.SemaphoreType.DMA((n_row + 1,)),
            pltpu.SemaphoreType.DMA((half, 2)),
            pltpu.SemaphoreType.DMA,
        ],
        compiler_params=pltpu.CompilerParams(
            collective_id=0, has_side_effects=True, vmem_limit_bytes=16 * 2**20
        ),
    )(
        *(
            pltpu.with_memory_space_constraint(operand, pltpu.HBM)
            for operand in (
                pair_rep,
                norm_gain.reshape(1, chan),
                norm_bias.reshape(1, chan),
                w_a_proj,
                w_a_gate,
                w_b_proj,
                w_b_gate,
                w_gate,
                out_gain.reshape(1, hidden),
                out_bias.reshape(1, hidden),
                w_out,
            )
        )
    )


def body(n_row, n_sub, *operands):
    rows, cols, _ = operands[0].shape
    hidden = operands[3].shape[1]
    gathered = cols * cols * n_sub * hidden * 2
    if n_sub == 2 and n_row % 2 == 0 and cols % 16 == 0 and gathered <= 4 * 2**20:
        return one_round(n_row, *operands)
    return per_device(*operands)


def solution(mesh):
    in_specs = (P(("grp", "row"), "sub", None), P(), P(), P(), P(), P(), P(), P(), P(), P(), P())
    out_specs = P(("grp", "row"), "sub", None)
    return jax.shard_map(
        functools.partial(body, mesh.shape["row"], mesh.shape["sub"]),
        mesh=mesh,
        in_specs=in_specs,
        out_specs=out_specs,
        check_vma=False,
    )
```

```python
import functools

import jax
import jax.numpy as jnp
from jax import lax
from jax.experimental import pallas as pl
from jax.experimental.pallas import tpu as pltpu
from jax.sharding import PartitionSpec as P

EPSILON = 1e-05


def layer_norm(values, gain, shift, axis):
    centred = values - jnp.mean(values, axis=axis, keepdims=True)
    variance = jnp.mean(centred * centred, axis=axis, keepdims=True)
    return centred * lax.rsqrt(variance + EPSILON) * gain + shift


def per_device(
    pair_rep,
    norm_gain,
    norm_bias,
    w_a_proj,
    w_a_gate,
    w_b_proj,
    w_b_gate,
    w_gate,
    out_gain,
    out_bias,
    w_out,
):
    hidden = w_a_proj.shape[1]
    w_inner = jnp.concatenate([w_a_proj, w_a_gate, w_b_proj, w_b_gate], axis=1)
    normed = layer_norm(pair_rep.astype(jnp.float32), norm_gain, norm_bias, -1).astype(jnp.bfloat16)
    inner = jnp.einsum("rkc,cm->mrk", normed, w_inner, preferred_element_type=jnp.float32)
    left_local = (jax.nn.sigmoid(inner[hidden : 2 * hidden]) * inner[:hidden]).astype(jnp.bfloat16)
    right_local = (
        jax.nn.sigmoid(inner[3 * hidden : 4 * hidden]) * inner[2 * hidden : 3 * hidden]
    ).astype(jnp.bfloat16)
    gating = jax.nn.sigmoid(
        jnp.einsum("rkc,cd->rkd", normed, w_gate, preferred_element_type=jnp.float32)
    ).astype(jnp.bfloat16)
    left_chan, right_chan = (
        lax.all_to_all(left_local, "row", split_axis=0, concat_axis=1, tiled=True),
        lax.all_to_all(right_local, "row", split_axis=0, concat_axis=1, tiled=True),
    )
    left_rows = lax.all_to_all(left_chan, "sub", split_axis=1, concat_axis=2, tiled=True)
    triangle = jnp.einsum(
        "hik,hjk->hij",
        left_rows,
        lax.all_gather(right_chan, "sub", axis=2, tiled=True),
        preferred_element_type=jnp.float32,
    ).astype(jnp.bfloat16)
    regrouped = lax.all_to_all(
        lax.all_to_all(triangle, "sub", split_axis=2, concat_axis=1, tiled=True),
        "row",
        split_axis=1,
        concat_axis=0,
        tiled=True,
    )
    hidden_normed = layer_norm(
        regrouped.astype(jnp.float32), out_gain[:, None, None], out_bias[:, None, None], 0
    ).astype(jnp.bfloat16)
    mixed = jnp.einsum("hrj,hc->rjc", hidden_normed, w_out, preferred_element_type=jnp.float32)
    return (gating.astype(jnp.float32) * mixed).astype(jnp.bfloat16)


def activations(normed, weights, hidden):
    inner = jnp.dot(normed, weights, preferred_element_type=jnp.float32)
    return (jax.nn.sigmoid(inner[:, hidden:]) * inner[:, :hidden]).astype(jnp.bfloat16)


def kernel(
    n_row,
    pair_hbm,
    ngain_hbm,
    nbias_hbm,
    wap_hbm,
    wag_hbm,
    wbp_hbm,
    wbg_hbm,
    wg_hbm,
    ogain_hbm,
    obias_hbm,
    wo_hbm,
    out_ref,
    raw,
    vec_v,
    w_v,
    wo_v,
    norm_v,
    tri_v,
    result,
    in_sem,
    send_sem,
    recv_sem,
    result_sem,
):
    _, _, rows, cols, chan = raw.shape
    hidden = tri_v.shape[-1]
    half = n_row // 2
    row = lax.axis_index("row")
    sub = lax.axis_index("sub")
    part = row // half
    place = lax.rem(row, half)
    mirror = lax.rem(row + half, n_row)
    near = sub == part
    far = jnp.logical_not(near)

    def remote(src, dst, send, recv, target_row, target_sub):
        return pltpu.make_async_remote_copy(
            src_ref=src,
            dst_ref=dst,
            send_sem=send,
            recv_sem=recv,
            device_id={"row": target_row, "sub": target_sub},
            device_id_type=pl.DeviceIdType.MESH,
        )

    loads = [
        pltpu.make_async_copy(ngain_hbm, vec_v.at[0], in_sem.at[0]),
        pltpu.make_async_copy(nbias_hbm, vec_v.at[1], in_sem.at[1]),
        pltpu.make_async_copy(wbp_hbm, w_v.at[:, 0:hidden], in_sem.at[2]),
        pltpu.make_async_copy(wbg_hbm, w_v.at[:, hidden : 2 * hidden], in_sem.at[3]),
        pltpu.make_async_copy(wap_hbm, w_v.at[:, 2 * hidden : 3 * hidden], in_sem.at[4]),
        pltpu.make_async_copy(wag_hbm, w_v.at[:, 3 * hidden : 4 * hidden], in_sem.at[5]),
        pltpu.make_async_copy(wg_hbm, w_v.at[:, 4 * hidden : 4 * hidden + chan], in_sem.at[6]),
        pltpu.make_async_copy(ogain_hbm, vec_v.at[2], in_sem.at[7]),
        pltpu.make_async_copy(obias_hbm, vec_v.at[3], in_sem.at[8]),
        pltpu.make_async_copy(wo_hbm, wo_v, in_sem.at[9]),
    ]
    own_load = pltpu.make_async_copy(pair_hbm, raw.at[place, sub], recv_sem.at[place, sub])

    barrier = pltpu.get_barrier_semaphore()

    def greet(target_row, target_sub):
        pl.semaphore_signal(
            barrier,
            inc=1,
            device_id={"row": target_row, "sub": target_sub},
            device_id_type=pl.DeviceIdType.MESH,
        )

    @pl.when(near)
    def _():
        greet(mirror, 0)
        greet(mirror, 1)
        for step in range(1, half):
            for source_sub in range(2):
                greet(part * half + lax.rem(place + step, half), source_sub)
        greet(row, 1 - sub)
        own_load.start()
        for load in loads:
            load.start()

    @pl.when(far)
    def _():
        greet(mirror, sub)

    pl.semaphore_wait(barrier, half + 1)

    to_mirror = remote(
        pair_hbm, raw.at[half, sub], send_sem.at[half], recv_sem.at[half, sub], mirror, 1 - part
    )
    to_near = [
        remote(
            pair_hbm,
            raw.at[place, sub],
            send_sem.at[step],
            recv_sem.at[place, sub],
            part * half + lax.rem(place + step, half),
            part,
        )
        for step in range(half)
    ]
    for step in range(half - 1, 0, -1):
        to_near[step].start()

    @pl.when(far)
    def _():
        to_near[0].start()

    to_mirror.start()
    send_result = remote(
        result, out_ref, send_sem.at[half + 1], result_sem, mirror, sub
    )

    @pl.when(near)
    def _():
        def arrive(unit):
            for source_sub in range(2):
                pltpu.make_async_copy(
                    pair_hbm, raw.at[unit, source_sub], recv_sem.at[unit, source_sub]
                ).wait()
            pair = raw[unit].astype(jnp.float32).reshape(2 * rows * cols, chan)
            return layer_norm(pair, vec_v[0], vec_v[1], -1).astype(jnp.bfloat16)

        def spread(act):
            return act.astype(jnp.float32).reshape(2, rows, cols, hidden)

        w_right = slice(0, 2 * hidden)
        w_left = slice(2 * hidden, 4 * hidden)
        for load in loads:
            load.wait()

        normed = arrive(place)
        norm_v[0] = normed.reshape(2, rows * cols, chan)
        rights = [spread(activations(normed, w_v[:, w_right], hidden))]
        lefts = [spread(activations(normed, w_v[:, w_left], hidden))]
        normed = arrive(half)
        norm_v[1] = normed.reshape(2, rows * cols, chan)
        lefts.append(spread(activations(normed, w_v[:, w_left], hidden)))
        gated = norm_v[:, sub].reshape(2 * rows * cols, chan)
        gating = jax.nn.sigmoid(
            jnp.dot(
                gated, w_v[:, 4 * hidden : 4 * hidden + chan], preferred_element_type=jnp.float32
            )
        ).astype(jnp.bfloat16)

        for step in range(half):
            unit = lax.rem(place + step, half)
            if step == 0:
                block = rights[0]
            else:
                block = spread(activations(arrive(unit), w_v[:, w_right], hidden))
            for which in range(2):
                for i in range(rows):
                    prod = lefts[which][:, i][:, None] * block
                    prod = prod[0] + prod[1]
                    prod = jnp.sum(prod.reshape(rows, cols // 8, 8, hidden), axis=1)
                    tri_v[which, i, unit] = jnp.sum(prod, axis=1)

        tri = jnp.concatenate(
            [
                tri_v[which, i, unit]
                for which in range(2)
                for i in range(rows)
                for unit in range(half)
            ],
            axis=0,
        )
        tri = tri.astype(jnp.bfloat16).astype(jnp.float32)
        hidden_normed = layer_norm(tri, vec_v[2], vec_v[3], -1).astype(jnp.bfloat16)
        mixed = jnp.dot(hidden_normed, wo_v[...], preferred_element_type=jnp.float32)
        out = (gating.astype(jnp.float32) * mixed).astype(jnp.bfloat16)
        out = out.reshape(2, rows, cols, chan)
        result[...] = out[1]
        send_result.start()
        out_ref[...] = out[0]
        send_result.wait_send()

    @pl.when(far)
    def _():
        send_result.wait_recv()
        to_near[0].wait_send()

    to_mirror.wait_send()
    for step in range(1, half):
        to_near[step].wait_send()


def one_round(n_row, pair_rep, norm_gain, norm_bias, *rest):
    w_a_proj, w_a_gate, w_b_proj, w_b_gate, w_gate, out_gain, out_bias, w_out = rest
    rows, cols, chan = pair_rep.shape
    hidden = w_a_proj.shape[1]
    half = n_row // 2
    hbm = pl.BlockSpec(memory_space=pltpu.HBM)
    return pl.pallas_call(
        functools.partial(kernel, n_row),
        out_shape=pltpu.VMEM((rows, cols, chan), jnp.bfloat16),
        in_specs=[hbm] * 11,
        out_specs=pl.BlockSpec(memory_space=pltpu.VMEM),
        scratch_shapes=[
            pltpu.VMEM((half + 1, 2, rows, cols, chan), jnp.bfloat16),
            pltpu.VMEM((4, 1, chan), jnp.float32),
            pltpu.VMEM((chan, 4 * hidden + chan), jnp.bfloat16),
            pltpu.VMEM((hidden, chan), jnp.bfloat16),
            pltpu.VMEM((2, 2, rows * cols, chan), jnp.bfloat16),
            pltpu.VMEM((2, rows, half, rows, hidden), jnp.float32),
            pltpu.VMEM((rows, cols, chan), jnp.bfloat16),
            pltpu.SemaphoreType.DMA((10,)),
            pltpu.SemaphoreType.DMA((half + 2,)),
            pltpu.SemaphoreType.DMA((half + 1, 2)),
            pltpu.SemaphoreType.DMA,
        ],
        compiler_params=pltpu.CompilerParams(
            collective_id=0, has_side_effects=True, vmem_limit_bytes=16 * 2**20
        ),
    )(
        *(
            pltpu.with_memory_space_constraint(operand, pltpu.HBM)
            for operand in (
                pair_rep,
                norm_gain.reshape(1, chan),
                norm_bias.reshape(1, chan),
                w_a_proj,
                w_a_gate,
                w_b_proj,
                w_b_gate,
                w_gate,
                out_gain.reshape(1, hidden),
                out_bias.reshape(1, hidden),
                w_out,
            )
        )
    )


def body(n_row, n_sub, *operands):
    rows, cols, _ = operands[0].shape
    hidden = operands[3].shape[1]
    gathered = cols * cols * n_sub * hidden * 2
    if n_sub == 2 and n_row % 2 == 0 and cols % 16 == 0 and gathered <= 4 * 2**20:
        return one_round(n_row, *operands)
    return per_device(*operands)


def solution(mesh):
    in_specs = (P(("grp", "row"), "sub", None), P(), P(), P(), P(), P(), P(), P(), P(), P(), P())
    out_specs = P(("grp", "row"), "sub", None)
    return jax.shard_map(
        functools.partial(body, mesh.shape["row"], mesh.shape["sub"]),
        mesh=mesh,
        in_specs=in_specs,
        out_specs=out_specs,
        check_vma=False,
    )
```

```python
import functools

import jax
import jax.numpy as jnp
from jax import lax
from jax.experimental import pallas as pl
from jax.experimental.pallas import tpu as pltpu
from jax.sharding import PartitionSpec as P

EPSILON = 1e-05


def layer_norm(values, gain, shift, axis):
    centred = values - jnp.mean(values, axis=axis, keepdims=True)
    variance = jnp.mean(centred * centred, axis=axis, keepdims=True)
    return centred * lax.rsqrt(variance + EPSILON) * gain + shift


def per_device(
    pair_rep,
    norm_gain,
    norm_bias,
    w_a_proj,
    w_a_gate,
    w_b_proj,
    w_b_gate,
    w_gate,
    out_gain,
    out_bias,
    w_out,
):
    hidden = w_a_proj.shape[1]
    w_inner = jnp.concatenate([w_a_proj, w_a_gate, w_b_proj, w_b_gate], axis=1)
    normed = layer_norm(pair_rep.astype(jnp.float32), norm_gain, norm_bias, -1).astype(jnp.bfloat16)
    inner = jnp.einsum("rkc,cm->mrk", normed, w_inner, preferred_element_type=jnp.float32)
    left_local = (jax.nn.sigmoid(inner[hidden : 2 * hidden]) * inner[:hidden]).astype(jnp.bfloat16)
    right_local = (
        jax.nn.sigmoid(inner[3 * hidden : 4 * hidden]) * inner[2 * hidden : 3 * hidden]
    ).astype(jnp.bfloat16)
    gating = jax.nn.sigmoid(
        jnp.einsum("rkc,cd->rkd", normed, w_gate, preferred_element_type=jnp.float32)
    ).astype(jnp.bfloat16)
    left_chan, right_chan = (
        lax.all_to_all(left_local, "row", split_axis=0, concat_axis=1, tiled=True),
        lax.all_to_all(right_local, "row", split_axis=0, concat_axis=1, tiled=True),
    )
    left_rows = lax.all_to_all(left_chan, "sub", split_axis=1, concat_axis=2, tiled=True)
    triangle = jnp.einsum(
        "hik,hjk->hij",
        left_rows,
        lax.all_gather(right_chan, "sub", axis=2, tiled=True),
        preferred_element_type=jnp.float32,
    ).astype(jnp.bfloat16)
    regrouped = lax.all_to_all(
        lax.all_to_all(triangle, "sub", split_axis=2, concat_axis=1, tiled=True),
        "row",
        split_axis=1,
        concat_axis=0,
        tiled=True,
    )
    hidden_normed = layer_norm(
        regrouped.astype(jnp.float32), out_gain[:, None, None], out_bias[:, None, None], 0
    ).astype(jnp.bfloat16)
    mixed = jnp.einsum("hrj,hc->rjc", hidden_normed, w_out, preferred_element_type=jnp.float32)
    return (gating.astype(jnp.float32) * mixed).astype(jnp.bfloat16)


def kernel(
    n_row,
    pair_hbm,
    ngain_hbm,
    nbias_hbm,
    wap_hbm,
    wag_hbm,
    wbp_hbm,
    wbg_hbm,
    wg_hbm,
    ogain_hbm,
    obias_hbm,
    wo_hbm,
    out_ref,
    pair_v,
    vec_v,
    w_v,
    wo_v,
    right_send,
    left_send,
    right_buf,
    left_buf,
    part_v,
    tri_send,
    tri_v,
    in_sem,
    send_sem,
    recv_sem,
    left_sem,
    tri_sem,
):
    rows, cols, chan = pair_v.shape
    hidden = right_buf.shape[-1]
    half = n_row // 2
    row = lax.axis_index("row")
    sub = lax.axis_index("sub")
    part = row // half
    place = lax.rem(row, half)
    mirror = lax.rem(row + half, n_row)
    near = sub == part
    far = jnp.logical_not(near)

    def remote(src, dst, send, recv, target_row, target_sub):
        return pltpu.make_async_remote_copy(
            src_ref=src,
            dst_ref=dst,
            send_sem=send,
            recv_sem=recv,
            device_id={"row": target_row, "sub": target_sub},
            device_id_type=pl.DeviceIdType.MESH,
        )

    loads = [
        pltpu.make_async_copy(pair_hbm, pair_v, in_sem.at[0]),
        pltpu.make_async_copy(ngain_hbm, vec_v.at[0], in_sem.at[1]),
        pltpu.make_async_copy(nbias_hbm, vec_v.at[1], in_sem.at[2]),
        pltpu.make_async_copy(wbp_hbm, w_v.at[:, 0:hidden], in_sem.at[3]),
        pltpu.make_async_copy(wbg_hbm, w_v.at[:, hidden : 2 * hidden], in_sem.at[4]),
        pltpu.make_async_copy(wap_hbm, w_v.at[:, 2 * hidden : 3 * hidden], in_sem.at[5]),
        pltpu.make_async_copy(wag_hbm, w_v.at[:, 3 * hidden : 4 * hidden], in_sem.at[6]),
        pltpu.make_async_copy(wg_hbm, w_v.at[:, 4 * hidden : 4 * hidden + chan], in_sem.at[7]),
        pltpu.make_async_copy(ogain_hbm, vec_v.at[2], in_sem.at[8]),
        pltpu.make_async_copy(obias_hbm, vec_v.at[3], in_sem.at[9]),
        pltpu.make_async_copy(wo_hbm, wo_v, in_sem.at[10]),
    ]
    for load in loads:
        load.start()

    barrier = pltpu.get_barrier_semaphore()

    def greet(target_row, target_sub):
        pl.semaphore_signal(
            barrier,
            inc=1,
            device_id={"row": target_row, "sub": target_sub},
            device_id_type=pl.DeviceIdType.MESH,
        )

    @pl.when(near)
    def _():
        greet(mirror, 0)
        greet(mirror, 1)
        for step in range(1, half):
            for source_sub in range(2):
                greet(part * half + lax.rem(place + step, half), source_sub)
        greet(row, 1 - sub)

    @pl.when(far)
    def _():
        greet(mirror, sub)

    for load in loads[:3]:
        load.wait()
    pair = pair_v[...].astype(jnp.float32).reshape(rows * cols, chan)
    normed = layer_norm(pair, vec_v[0], vec_v[1], -1).astype(jnp.bfloat16)
    for load in loads[3:7]:
        load.wait()
    inner = jnp.dot(normed, w_v[:, 0 : 4 * hidden], preferred_element_type=jnp.float32)
    right = jax.nn.sigmoid(inner[:, hidden : 2 * hidden]) * inner[:, :hidden]
    left = jax.nn.sigmoid(inner[:, 3 * hidden :]) * inner[:, 2 * hidden : 3 * hidden]
    right = right.astype(jnp.bfloat16).reshape(rows, cols, hidden)
    left = left.astype(jnp.bfloat16).reshape(rows, cols, hidden)
    right_send[...] = right
    left_send[...] = left

    @pl.when(near)
    def _():
        right_buf[place, sub] = right
        left_buf[0, sub] = left

    pl.semaphore_wait(barrier, half + 1)

    left_to_mirror = remote(
        left_send,
        left_buf.at[1, sub],
        send_sem.at[half],
        left_sem.at[1, sub],
        mirror,
        1 - part,
    )
    left_to_near = remote(
        left_send, left_buf.at[0, sub], send_sem.at[half + 1], left_sem.at[0, sub], row, part
    )
    right_to_near = [
        remote(
            right_send,
            right_buf.at[place, sub],
            send_sem.at[step],
            recv_sem.at[place, sub],
            part * half + lax.rem(place + step, half),
            part,
        )
        for step in range(half)
    ]
    left_to_mirror.start()
    for step in range(half - 1, 0, -1):
        right_to_near[step].start()

    @pl.when(far)
    def _():
        right_to_near[0].start()
        left_to_near.start()

    loads[7].wait()
    gating = jax.nn.sigmoid(
        jnp.dot(
            normed, w_v[:, 4 * hidden : 4 * hidden + chan], preferred_element_type=jnp.float32
        )
    ).astype(jnp.bfloat16)
    for load in loads[8:]:
        load.wait()

    send_tri = remote(tri_send, tri_v, send_sem.at[half + 2], tri_sem, mirror, sub)

    @pl.when(near)
    def _():
        def arrived(buffer, semaphore):
            pltpu.make_async_copy(right_send, buffer, semaphore).wait()

        arrived(left_buf.at[0, 1 - sub], left_sem.at[0, 1 - sub])
        for source_sub in range(2):
            arrived(left_buf.at[1, source_sub], left_sem.at[1, source_sub])
        lefts = [left_buf[which].astype(jnp.float32) for which in range(2)]
        for step in range(half):
            unit = lax.rem(place + step, half)
            if step == 0:
                arrived(right_buf.at[unit, 1 - sub], recv_sem.at[unit, 1 - sub])
            else:
                for source_sub in range(2):
                    arrived(right_buf.at[unit, source_sub], recv_sem.at[unit, source_sub])
            block = right_buf[unit].astype(jnp.float32)
            for which in (1, 0):
                for i in range(rows):
                    prod = lefts[which][:, i][:, None] * block
                    prod = prod[0] + prod[1]
                    prod = jnp.sum(prod.reshape(rows, cols // 8, 8, hidden), axis=1)
                    part_v[which, i, unit] = jnp.sum(prod, axis=1)

        def gathered(which):
            pieces = [part_v[which, i, unit] for i in range(rows) for unit in range(half)]
            whole = jnp.concatenate(pieces, axis=0).astype(jnp.bfloat16)
            return whole.reshape(rows, cols, hidden)

        tri_send[...] = gathered(1)
        send_tri.start()
        tri_v[...] = gathered(0)

    @pl.when(far)
    def _():
        send_tri.wait_recv()

    tri = tri_v[...].reshape(rows * cols, hidden).astype(jnp.float32)
    hidden_normed = layer_norm(tri, vec_v[2], vec_v[3], -1).astype(jnp.bfloat16)
    mixed = jnp.dot(hidden_normed, wo_v[...], preferred_element_type=jnp.float32)
    out = (gating.astype(jnp.float32) * mixed).astype(jnp.bfloat16)
    out_ref[...] = out.reshape(rows, cols, chan)

    left_to_mirror.wait_send()
    for step in range(1, half):
        right_to_near[step].wait_send()

    @pl.when(far)
    def _():
        right_to_near[0].wait_send()
        left_to_near.wait_send()

    @pl.when(near)
    def _():
        send_tri.wait_send()


def one_round(n_row, pair_rep, norm_gain, norm_bias, *rest):
    w_a_proj, w_a_gate, w_b_proj, w_b_gate, w_gate, out_gain, out_bias, w_out = rest
    rows, cols, chan = pair_rep.shape
    hidden = w_a_proj.shape[1]
    half = n_row // 2
    hbm = pl.BlockSpec(memory_space=pltpu.HBM)
    return pl.pallas_call(
        functools.partial(kernel, n_row),
        out_shape=pltpu.VMEM((rows, cols, chan), jnp.bfloat16),
        in_specs=[hbm] * 11,
        out_specs=pl.BlockSpec(memory_space=pltpu.VMEM),
        scratch_shapes=[
            pltpu.VMEM((rows, cols, chan), jnp.bfloat16),
            pltpu.VMEM((4, 1, chan), jnp.float32),
            pltpu.VMEM((chan, 4 * hidden + chan), jnp.bfloat16),
            pltpu.VMEM((hidden, chan), jnp.bfloat16),
            pltpu.VMEM((rows, cols, hidden), jnp.bfloat16),
            pltpu.VMEM((rows, cols, hidden), jnp.bfloat16),
            pltpu.VMEM((half, 2, rows, cols, hidden), jnp.bfloat16),
            pltpu.VMEM((2, 2, rows, cols, hidden), jnp.bfloat16),
            pltpu.VMEM((2, rows, half, rows, hidden), jnp.float32),
            pltpu.VMEM((rows, cols, hidden), jnp.bfloat16),
            pltpu.VMEM((rows, cols, hidden), jnp.bfloat16),
            pltpu.SemaphoreType.DMA((11,)),
            pltpu.SemaphoreType.DMA((half + 3,)),
            pltpu.SemaphoreType.DMA((half, 2)),
            pltpu.SemaphoreType.DMA((2, 2)),
            pltpu.SemaphoreType.DMA,
        ],
        compiler_params=pltpu.CompilerParams(
            collective_id=0, has_side_effects=True, vmem_limit_bytes=16 * 2**20
        ),
    )(
        *(
            pltpu.with_memory_space_constraint(operand, pltpu.HBM)
            for operand in (
                pair_rep,
                norm_gain.reshape(1, chan),
                norm_bias.reshape(1, chan),
                w_a_proj,
                w_a_gate,
                w_b_proj,
                w_b_gate,
                w_gate,
                out_gain.reshape(1, hidden),
                out_bias.reshape(1, hidden),
                w_out,
            )
        )
    )


def body(n_row, n_sub, *operands):
    rows, cols, _ = operands[0].shape
    hidden = operands[3].shape[1]
    gathered = cols * cols * n_sub * hidden * 2
    if n_sub == 2 and n_row % 2 == 0 and cols % 16 == 0 and gathered <= 4 * 2**20:
        return one_round(n_row, *operands)
    return per_device(*operands)


def solution(mesh):
    in_specs = (P(("grp", "row"), "sub", None), P(), P(), P(), P(), P(), P(), P(), P(), P(), P())
    out_specs = P(("grp", "row"), "sub", None)
    return jax.shard_map(
        functools.partial(body, mesh.shape["row"], mesh.shape["sub"]),
        mesh=mesh,
        in_specs=in_specs,
        out_specs=out_specs,
        check_vma=False,
    )
```

```python
import functools

import jax
import jax.numpy as jnp
from jax import lax
from jax.experimental import pallas as pl
from jax.experimental.pallas import tpu as pltpu
from jax.sharding import PartitionSpec as P

EPSILON = 1e-05


def layer_norm(values, gain, shift, axis):
    centred = values - jnp.mean(values, axis=axis, keepdims=True)
    variance = jnp.mean(centred * centred, axis=axis, keepdims=True)
    return centred * lax.rsqrt(variance + EPSILON) * gain + shift


def per_device(
    pair_rep,
    norm_gain,
    norm_bias,
    w_a_proj,
    w_a_gate,
    w_b_proj,
    w_b_gate,
    w_gate,
    out_gain,
    out_bias,
    w_out,
):
    hidden = w_a_proj.shape[1]
    w_inner = jnp.concatenate([w_a_proj, w_a_gate, w_b_proj, w_b_gate], axis=1)
    normed = layer_norm(pair_rep.astype(jnp.float32), norm_gain, norm_bias, -1).astype(jnp.bfloat16)
    inner = jnp.einsum("rkc,cm->mrk", normed, w_inner, preferred_element_type=jnp.float32)
    left_local = (jax.nn.sigmoid(inner[hidden : 2 * hidden]) * inner[:hidden]).astype(jnp.bfloat16)
    right_local = (
        jax.nn.sigmoid(inner[3 * hidden : 4 * hidden]) * inner[2 * hidden : 3 * hidden]
    ).astype(jnp.bfloat16)
    gating = jax.nn.sigmoid(
        jnp.einsum("rkc,cd->rkd", normed, w_gate, preferred_element_type=jnp.float32)
    ).astype(jnp.bfloat16)
    left_chan, right_chan = (
        lax.all_to_all(left_local, "row", split_axis=0, concat_axis=1, tiled=True),
        lax.all_to_all(right_local, "row", split_axis=0, concat_axis=1, tiled=True),
    )
    left_rows = lax.all_to_all(left_chan, "sub", split_axis=1, concat_axis=2, tiled=True)
    triangle = jnp.einsum(
        "hik,hjk->hij",
        left_rows,
        lax.all_gather(right_chan, "sub", axis=2, tiled=True),
        preferred_element_type=jnp.float32,
    ).astype(jnp.bfloat16)
    regrouped = lax.all_to_all(
        lax.all_to_all(triangle, "sub", split_axis=2, concat_axis=1, tiled=True),
        "row",
        split_axis=1,
        concat_axis=0,
        tiled=True,
    )
    hidden_normed = layer_norm(
        regrouped.astype(jnp.float32), out_gain[:, None, None], out_bias[:, None, None], 0
    ).astype(jnp.bfloat16)
    mixed = jnp.einsum("hrj,hc->rjc", hidden_normed, w_out, preferred_element_type=jnp.float32)
    return (gating.astype(jnp.float32) * mixed).astype(jnp.bfloat16)


def kernel(
    n_row,
    pair_hbm,
    ngain_hbm,
    nbias_hbm,
    wap_hbm,
    wag_hbm,
    wbp_hbm,
    wbg_hbm,
    wg_hbm,
    ogain_hbm,
    obias_hbm,
    wo_hbm,
    out_ref,
    pair_v,
    vec_v,
    w_v,
    wo_v,
    right_send,
    right_buf,
    left_buf,
    tri_v,
    in_sem,
    send_sem,
    recv_sem,
    left_sem,
    ready,
):
    rows, cols, chan = pair_v.shape
    hidden = right_send.shape[-1]
    half = n_row // 2
    row = lax.axis_index("row")
    sub = lax.axis_index("sub")
    other = 1 - sub
    owner = row // half
    slot = lax.rem(row, half)
    near = sub == owner
    low = owner == 0

    loads = [
        pltpu.make_async_copy(pair_hbm, pair_v, in_sem.at[0]),
        pltpu.make_async_copy(ngain_hbm, vec_v.at[0], in_sem.at[1]),
        pltpu.make_async_copy(nbias_hbm, vec_v.at[1], in_sem.at[2]),
        pltpu.make_async_copy(wbp_hbm, w_v.at[:, 0:hidden], in_sem.at[3]),
        pltpu.make_async_copy(wbg_hbm, w_v.at[:, hidden : 2 * hidden], in_sem.at[4]),
        pltpu.make_async_copy(wap_hbm, w_v.at[:, 2 * hidden : 3 * hidden], in_sem.at[5]),
        pltpu.make_async_copy(wag_hbm, w_v.at[:, 3 * hidden : 4 * hidden], in_sem.at[6]),
        pltpu.make_async_copy(wg_hbm, w_v.at[:, 4 * hidden : 4 * hidden + chan], in_sem.at[7]),
        pltpu.make_async_copy(ogain_hbm, vec_v.at[2], in_sem.at[8]),
        pltpu.make_async_copy(obias_hbm, vec_v.at[3], in_sem.at[9]),
        pltpu.make_async_copy(wo_hbm, wo_v, in_sem.at[10]),
    ]
    for load in loads:
        load.start()

    barrier = pltpu.get_barrier_semaphore()

    def greet(semaphore, target_row, target_sub):
        pl.semaphore_signal(
            semaphore,
            inc=1,
            device_id={"row": target_row, "sub": target_sub},
            device_id_type=pl.DeviceIdType.MESH,
        )

    @pl.when(low)
    def _():
        for step in range(half):
            greet(barrier, half + step, 0)

            @pl.when(sub == 1)
            def _():
                greet(barrier, half + step, 1)

    @pl.when(near)
    def _():
        for step in range(1, half):
            for source_sub in range(2):
                greet(barrier, owner * half + lax.rem(slot + step, half), source_sub)

    greet(barrier, row, other)

    for load in loads[:3]:
        load.wait()
    pair = pair_v[...].astype(jnp.float32).reshape(rows * cols, chan)
    normed = layer_norm(pair, vec_v[0], vec_v[1], -1).astype(jnp.bfloat16)
    for load in loads[3:5]:
        load.wait()
    inner = jnp.dot(normed, w_v[:, 0 : 2 * hidden], preferred_element_type=jnp.float32)
    right = jax.nn.sigmoid(inner[:, hidden:]) * inner[:, :hidden]
    right = right.astype(jnp.bfloat16).reshape(rows, cols, hidden)
    right_send[...] = right

    @pl.when(owner == sub)
    def _():
        right_buf[slot, sub] = right

    for load in loads[5:7]:
        load.wait()
    inner = jnp.dot(
        normed, w_v[:, 2 * hidden : 4 * hidden], preferred_element_type=jnp.float32
    )
    left = jax.nn.sigmoid(inner[:, hidden:]) * inner[:, :hidden]
    left_buf[sub] = left.astype(jnp.bfloat16).reshape(rows, cols, hidden)

    pl.semaphore_wait(barrier, half + owner * half * (2 - sub))

    left_copy = pltpu.make_async_remote_copy(
        src_ref=left_buf.at[sub],
        dst_ref=left_buf.at[sub],
        send_sem=send_sem.at[n_row],
        recv_sem=left_sem,
        device_id={"sub": other},
        device_id_type=pl.DeviceIdType.MESH,
    )

    def right_copy(index, target):
        return pltpu.make_async_remote_copy(
            src_ref=right_send,
            dst_ref=right_buf.at[slot, sub],
            send_sem=send_sem.at[index],
            recv_sem=recv_sem.at[slot, sub],
            device_id={"row": target, "sub": owner},
            device_id_type=pl.DeviceIdType.MESH,
        )

    inside = [right_copy(q, owner * half + q) for q in range(half)]
    across = [right_copy(half + q, (1 - owner) * half + q) for q in range(half)]

    def send_across():
        for copy in across:
            copy.start()

    def ready_then_across():
        pl.semaphore_wait(ready, half)
        send_across()

    @pl.when(jnp.logical_not(low))
    def _():
        send_across()

        @pl.when(sub == 0)
        def _():
            for step in range(half):
                for source_sub in range(2):
                    greet(ready, step, source_sub)

    for q in range(half):

        @pl.when(jnp.logical_not(jnp.logical_and(near, slot == q)))
        def _():
            inside[q].start()

    left_copy.start()

    @pl.when(jnp.logical_and(low, jnp.logical_not(near)))
    def _():
        ready_then_across()

    loads[7].wait()
    gating = jax.nn.sigmoid(
        jnp.dot(
            normed, w_v[:, 4 * hidden : 4 * hidden + chan], preferred_element_type=jnp.float32
        )
    ).astype(jnp.bfloat16)
    for load in loads[8:]:
        load.wait()

    left_copy.wait_recv()
    left_all = left_buf[...].astype(jnp.float32)
    for source in range(half):
        for source_sub in range(2):
            mine = jnp.logical_and(sub * half + source == row, sub == source_sub)

            @pl.when(jnp.logical_not(mine))
            def _():
                pltpu.make_async_remote_copy(
                    src_ref=right_send,
                    dst_ref=right_buf.at[source, source_sub],
                    send_sem=send_sem.at[0],
                    recv_sem=recv_sem.at[source, source_sub],
                    device_id={"sub": other},
                    device_id_type=pl.DeviceIdType.MESH,
                ).wait_recv()

        block = right_buf[source].astype(jnp.float32)
        for i in range(rows):
            prod = left_all[:, i][:, None] * block
            prod = prod[0] + prod[1]
            prod = jnp.sum(prod.reshape(rows, cols // 8, 8, hidden), axis=1)
            tri_v[i, source * rows : (source + 1) * rows, :] = jnp.sum(prod, axis=1)

    tri = tri_v[...].reshape(rows * cols, hidden).astype(jnp.bfloat16).astype(jnp.float32)
    hidden_normed = layer_norm(tri, vec_v[2], vec_v[3], -1).astype(jnp.bfloat16)
    mixed = jnp.dot(hidden_normed, wo_v[...], preferred_element_type=jnp.float32)
    out = (gating.astype(jnp.float32) * mixed).astype(jnp.bfloat16)
    out_ref[...] = out.reshape(rows, cols, chan)

    @pl.when(jnp.logical_and(low, near))
    def _():
        ready_then_across()

    left_copy.wait_send()
    for q in range(half):

        @pl.when(jnp.logical_not(jnp.logical_and(near, slot == q)))
        def _():
            inside[q].wait_send()

        across[q].wait_send()


def one_round(n_row, pair_rep, norm_gain, norm_bias, *rest):
    w_a_proj, w_a_gate, w_b_proj, w_b_gate, w_gate, out_gain, out_bias, w_out = rest
    rows, cols, chan = pair_rep.shape
    hidden = w_a_proj.shape[1]
    half = n_row // 2
    hbm = pl.BlockSpec(memory_space=pltpu.HBM)
    return pl.pallas_call(
        functools.partial(kernel, n_row),
        out_shape=pltpu.VMEM((rows, cols, chan), jnp.bfloat16),
        in_specs=[hbm] * 11,
        out_specs=pl.BlockSpec(memory_space=pltpu.VMEM),
        scratch_shapes=[
            pltpu.VMEM((rows, cols, chan), jnp.bfloat16),
            pltpu.VMEM((4, 1, chan), jnp.float32),
            pltpu.VMEM((chan, 4 * hidden + chan), jnp.bfloat16),
            pltpu.VMEM((hidden, chan), jnp.bfloat16),
            pltpu.VMEM((rows, cols, hidden), jnp.bfloat16),
            pltpu.VMEM((half, 2, rows, cols, hidden), jnp.bfloat16),
            pltpu.VMEM((2, rows, cols, hidden), jnp.bfloat16),
            pltpu.VMEM((rows, cols, hidden), jnp.float32),
            pltpu.SemaphoreType.DMA((11,)),
            pltpu.SemaphoreType.DMA((n_row + 1,)),
            pltpu.SemaphoreType.DMA((half, 2)),
            pltpu.SemaphoreType.DMA,
            pltpu.SemaphoreType.REGULAR,
        ],
        compiler_params=pltpu.CompilerParams(
            collective_id=0, has_side_effects=True, vmem_limit_bytes=16 * 2**20
        ),
    )(
        *(
            pltpu.with_memory_space_constraint(operand, pltpu.HBM)
            for operand in (
                pair_rep,
                norm_gain.reshape(1, chan),
                norm_bias.reshape(1, chan),
                w_a_proj,
                w_a_gate,
                w_b_proj,
                w_b_gate,
                w_gate,
                out_gain.reshape(1, hidden),
                out_bias.reshape(1, hidden),
                w_out,
            )
        )
    )


def body(n_row, n_sub, *operands):
    rows, cols, _ = operands[0].shape
    hidden = operands[3].shape[1]
    gathered = cols * cols * n_sub * hidden * 2
    if n_sub == 2 and n_row % 2 == 0 and cols % 16 == 0 and gathered <= 4 * 2**20:
        return one_round(n_row, *operands)
    return per_device(*operands)


def solution(mesh):
    in_specs = (P(("grp", "row"), "sub", None), P(), P(), P(), P(), P(), P(), P(), P(), P(), P())
    out_specs = P(("grp", "row"), "sub", None)
    return jax.shard_map(
        functools.partial(body, mesh.shape["row"], mesh.shape["sub"]),
        mesh=mesh,
        in_specs=in_specs,
        out_specs=out_specs,
        check_vma=False,
    )
```

```python
import functools

import jax
import jax.numpy as jnp
from jax import lax
from jax.experimental import pallas as pl
from jax.experimental.pallas import tpu as pltpu
from jax.sharding import PartitionSpec as P

EPSILON = 1e-05


def layer_norm(values, gain, shift, axis):
    centred = values - jnp.mean(values, axis=axis, keepdims=True)
    variance = jnp.mean(centred * centred, axis=axis, keepdims=True)
    return centred * lax.rsqrt(variance + EPSILON) * gain + shift


def per_device(
    pair_rep,
    norm_gain,
    norm_bias,
    w_a_proj,
    w_a_gate,
    w_b_proj,
    w_b_gate,
    w_gate,
    out_gain,
    out_bias,
    w_out,
):
    hidden = w_a_proj.shape[1]
    w_inner = jnp.concatenate([w_a_proj, w_a_gate, w_b_proj, w_b_gate], axis=1)
    normed = layer_norm(pair_rep.astype(jnp.float32), norm_gain, norm_bias, -1).astype(jnp.bfloat16)
    inner = jnp.einsum("rkc,cm->mrk", normed, w_inner, preferred_element_type=jnp.float32)
    left_local = (jax.nn.sigmoid(inner[hidden : 2 * hidden]) * inner[:hidden]).astype(jnp.bfloat16)
    right_local = (
        jax.nn.sigmoid(inner[3 * hidden : 4 * hidden]) * inner[2 * hidden : 3 * hidden]
    ).astype(jnp.bfloat16)
    gating = jax.nn.sigmoid(
        jnp.einsum("rkc,cd->rkd", normed, w_gate, preferred_element_type=jnp.float32)
    ).astype(jnp.bfloat16)
    left_chan, right_chan = (
        lax.all_to_all(left_local, "row", split_axis=0, concat_axis=1, tiled=True),
        lax.all_to_all(right_local, "row", split_axis=0, concat_axis=1, tiled=True),
    )
    left_rows = lax.all_to_all(left_chan, "sub", split_axis=1, concat_axis=2, tiled=True)
    triangle = jnp.einsum(
        "hik,hjk->hij",
        left_rows,
        lax.all_gather(right_chan, "sub", axis=2, tiled=True),
        preferred_element_type=jnp.float32,
    ).astype(jnp.bfloat16)
    regrouped = lax.all_to_all(
        lax.all_to_all(triangle, "sub", split_axis=2, concat_axis=1, tiled=True),
        "row",
        split_axis=1,
        concat_axis=0,
        tiled=True,
    )
    hidden_normed = layer_norm(
        regrouped.astype(jnp.float32), out_gain[:, None, None], out_bias[:, None, None], 0
    ).astype(jnp.bfloat16)
    mixed = jnp.einsum("hrj,hc->rjc", hidden_normed, w_out, preferred_element_type=jnp.float32)
    return (gating.astype(jnp.float32) * mixed).astype(jnp.bfloat16)


def kernel(
    n_row,
    pair_hbm,
    ngain_hbm,
    nbias_hbm,
    wap_hbm,
    wag_hbm,
    wbp_hbm,
    wbg_hbm,
    wg_hbm,
    ogain_hbm,
    obias_hbm,
    wo_hbm,
    out_ref,
    pair_v,
    vec_v,
    w_v,
    wo_v,
    right_send,
    right_buf,
    left_buf,
    tri_v,
    in_sem,
    send_sem,
    recv_sem,
    left_sem,
    ready,
):
    rows, cols, chan = pair_v.shape
    hidden = right_send.shape[-1]
    half = n_row // 2
    row = lax.axis_index("row")
    sub = lax.axis_index("sub")
    other = 1 - sub
    owner = row // half
    slot = lax.rem(row, half)
    near = sub == owner
    low = owner == 0
    high_near = jnp.logical_and(near, jnp.logical_not(low))
    high_far = jnp.logical_not(jnp.logical_or(near, low))

    loads = [
        pltpu.make_async_copy(pair_hbm, pair_v, in_sem.at[0]),
        pltpu.make_async_copy(ngain_hbm, vec_v.at[0], in_sem.at[1]),
        pltpu.make_async_copy(nbias_hbm, vec_v.at[1], in_sem.at[2]),
        pltpu.make_async_copy(wbp_hbm, w_v.at[:, 0:hidden], in_sem.at[3]),
        pltpu.make_async_copy(wbg_hbm, w_v.at[:, hidden : 2 * hidden], in_sem.at[4]),
        pltpu.make_async_copy(wap_hbm, w_v.at[:, 2 * hidden : 3 * hidden], in_sem.at[5]),
        pltpu.make_async_copy(wag_hbm, w_v.at[:, 3 * hidden : 4 * hidden], in_sem.at[6]),
        pltpu.make_async_copy(wg_hbm, w_v.at[:, 4 * hidden : 4 * hidden + chan], in_sem.at[7]),
        pltpu.make_async_copy(ogain_hbm, vec_v.at[2], in_sem.at[8]),
        pltpu.make_async_copy(obias_hbm, vec_v.at[3], in_sem.at[9]),
        pltpu.make_async_copy(wo_hbm, wo_v, in_sem.at[10]),
    ]
    for load in loads:
        load.start()

    barrier = pltpu.get_barrier_semaphore()

    def greet(semaphore, target_row, target_sub):
        pl.semaphore_signal(
            semaphore,
            inc=1,
            device_id={"row": target_row, "sub": target_sub},
            device_id_type=pl.DeviceIdType.MESH,
        )

    @pl.when(low)
    def _():
        for step in range(half):
            greet(barrier, half + step, 0)

            @pl.when(sub == 1)
            def _():
                greet(barrier, half + step, 1)

    @pl.when(near)
    def _():
        for step in range(1, half):
            greet(barrier, owner * half + lax.rem(slot + step, half), owner)

    @pl.when(low)
    def _():
        greet(barrier, row, other)

        @pl.when(near)
        def _():
            for step in range(1, half):
                greet(barrier, lax.rem(slot + step, half), 1)

    @pl.when(high_far)
    def _():
        for step in range(half):
            greet(barrier, half + step, 1)
        pl.semaphore_wait(barrier, 2 * half)
        for step in range(half):
            for source_sub in range(2):
                greet(ready, step, source_sub)

    for load in loads[:3]:
        load.wait()
    pair = pair_v[...].astype(jnp.float32).reshape(rows * cols, chan)
    normed = layer_norm(pair, vec_v[0], vec_v[1], -1).astype(jnp.bfloat16)
    for load in loads[3:5]:
        load.wait()
    inner = jnp.dot(normed, w_v[:, 0 : 2 * hidden], preferred_element_type=jnp.float32)
    right = jax.nn.sigmoid(inner[:, hidden:]) * inner[:, :hidden]
    right = right.astype(jnp.bfloat16).reshape(rows, cols, hidden)
    right_send[...] = right

    @pl.when(owner == sub)
    def _():
        right_buf[slot, sub] = right

    for load in loads[5:7]:
        load.wait()
    inner = jnp.dot(
        normed, w_v[:, 2 * hidden : 4 * hidden], preferred_element_type=jnp.float32
    )
    left = jax.nn.sigmoid(inner[:, hidden:]) * inner[:, :hidden]
    left_buf[sub] = left.astype(jnp.bfloat16).reshape(rows, cols, hidden)

    @pl.when(low)
    def _():
        pl.semaphore_wait(barrier, half)

    @pl.when(high_near)
    def _():
        pl.semaphore_wait(barrier, 3 * half - 1)

    left_copy = pltpu.make_async_remote_copy(
        src_ref=left_buf.at[sub],
        dst_ref=left_buf.at[sub],
        send_sem=send_sem.at[n_row],
        recv_sem=left_sem,
        device_id={"sub": other},
        device_id_type=pl.DeviceIdType.MESH,
    )

    def right_copy(index, target):
        return pltpu.make_async_remote_copy(
            src_ref=right_send,
            dst_ref=right_buf.at[slot, sub],
            send_sem=send_sem.at[index],
            recv_sem=recv_sem.at[slot, sub],
            device_id={"row": target, "sub": owner},
            device_id_type=pl.DeviceIdType.MESH,
        )

    inside = [right_copy(q, owner * half + q) for q in range(half)]
    across = [right_copy(half + q, (1 - owner) * half + q) for q in range(half)]

    def send_across():
        for copy in across:
            copy.start()

    @pl.when(jnp.logical_not(low))
    def _():
        send_across()

    @pl.when(high_near)
    def _():
        for step in range(half):
            greet(ready, half + step, 0)

    @pl.when(high_far)
    def _():
        pl.semaphore_wait(ready, half)

    for q in range(half):

        @pl.when(jnp.logical_not(jnp.logical_and(near, slot == q)))
        def _():
            inside[q].start()

    left_copy.start()

    @pl.when(low)
    def _():
        pl.semaphore_wait(ready, half)
        send_across()

    loads[7].wait()
    gating = jax.nn.sigmoid(
        jnp.dot(
            normed, w_v[:, 4 * hidden : 4 * hidden + chan], preferred_element_type=jnp.float32
        )
    ).astype(jnp.bfloat16)
    for load in loads[8:]:
        load.wait()

    left_copy.wait_recv()
    left_all = left_buf[...].astype(jnp.float32)
    for source in range(half):
        for source_sub in range(2):
            mine = jnp.logical_and(sub * half + source == row, sub == source_sub)

            @pl.when(jnp.logical_not(mine))
            def _():
                pltpu.make_async_remote_copy(
                    src_ref=right_send,
                    dst_ref=right_buf.at[source, source_sub],
                    send_sem=send_sem.at[0],
                    recv_sem=recv_sem.at[source, source_sub],
                    device_id={"sub": other},
                    device_id_type=pl.DeviceIdType.MESH,
                ).wait_recv()

        block = right_buf[source].astype(jnp.float32)
        for i in range(rows):
            prod = left_all[:, i][:, None] * block
            prod = prod[0] + prod[1]
            prod = jnp.sum(prod.reshape(rows, cols // 8, 8, hidden), axis=1)
            tri_v[i, source * rows : (source + 1) * rows, :] = jnp.sum(prod, axis=1)

    tri = tri_v[...].reshape(rows * cols, hidden).astype(jnp.bfloat16).astype(jnp.float32)
    hidden_normed = layer_norm(tri, vec_v[2], vec_v[3], -1).astype(jnp.bfloat16)
    mixed = jnp.dot(hidden_normed, wo_v[...], preferred_element_type=jnp.float32)
    out = (gating.astype(jnp.float32) * mixed).astype(jnp.bfloat16)
    out_ref[...] = out.reshape(rows, cols, chan)

    left_copy.wait_send()
    for q in range(half):

        @pl.when(jnp.logical_not(jnp.logical_and(near, slot == q)))
        def _():
            inside[q].wait_send()

        across[q].wait_send()


def one_round(n_row, pair_rep, norm_gain, norm_bias, *rest):
    w_a_proj, w_a_gate, w_b_proj, w_b_gate, w_gate, out_gain, out_bias, w_out = rest
    rows, cols, chan = pair_rep.shape
    hidden = w_a_proj.shape[1]
    half = n_row // 2
    hbm = pl.BlockSpec(memory_space=pltpu.HBM)
    return pl.pallas_call(
        functools.partial(kernel, n_row),
        out_shape=pltpu.VMEM((rows, cols, chan), jnp.bfloat16),
        in_specs=[hbm] * 11,
        out_specs=pl.BlockSpec(memory_space=pltpu.VMEM),
        scratch_shapes=[
            pltpu.VMEM((rows, cols, chan), jnp.bfloat16),
            pltpu.VMEM((4, 1, chan), jnp.float32),
            pltpu.VMEM((chan, 4 * hidden + chan), jnp.bfloat16),
            pltpu.VMEM((hidden, chan), jnp.bfloat16),
            pltpu.VMEM((rows, cols, hidden), jnp.bfloat16),
            pltpu.VMEM((half, 2, rows, cols, hidden), jnp.bfloat16),
            pltpu.VMEM((2, rows, cols, hidden), jnp.bfloat16),
            pltpu.VMEM((rows, cols, hidden), jnp.float32),
            pltpu.SemaphoreType.DMA((11,)),
            pltpu.SemaphoreType.DMA((n_row + 1,)),
            pltpu.SemaphoreType.DMA((half, 2)),
            pltpu.SemaphoreType.DMA,
            pltpu.SemaphoreType.REGULAR,
        ],
        compiler_params=pltpu.CompilerParams(
            collective_id=0, has_side_effects=True, vmem_limit_bytes=16 * 2**20
        ),
    )(
        *(
            pltpu.with_memory_space_constraint(operand, pltpu.HBM)
            for operand in (
                pair_rep,
                norm_gain.reshape(1, chan),
                norm_bias.reshape(1, chan),
                w_a_proj,
                w_a_gate,
                w_b_proj,
                w_b_gate,
                w_gate,
                out_gain.reshape(1, hidden),
                out_bias.reshape(1, hidden),
                w_out,
            )
        )
    )


def body(n_row, n_sub, *operands):
    rows, cols, _ = operands[0].shape
    hidden = operands[3].shape[1]
    gathered = cols * cols * n_sub * hidden * 2
    if n_sub == 2 and n_row % 2 == 0 and cols % 16 == 0 and gathered <= 4 * 2**20:
        return one_round(n_row, *operands)
    return per_device(*operands)


def solution(mesh):
    in_specs = (P(("grp", "row"), "sub", None), P(), P(), P(), P(), P(), P(), P(), P(), P(), P())
    out_specs = P(("grp", "row"), "sub", None)
    return jax.shard_map(
        functools.partial(body, mesh.shape["row"], mesh.shape["sub"]),
        mesh=mesh,
        in_specs=in_specs,
        out_specs=out_specs,
        check_vma=False,
    )
```

```python
import functools

import jax
import jax.numpy as jnp
from jax import lax
from jax.experimental import pallas as pl
from jax.experimental.pallas import tpu as pltpu
from jax.sharding import PartitionSpec as P

EPSILON = 1e-05


def layer_norm(values, gain, shift, axis):
    centred = values - jnp.mean(values, axis=axis, keepdims=True)
    variance = jnp.mean(centred * centred, axis=axis, keepdims=True)
    return centred * lax.rsqrt(variance + EPSILON) * gain + shift


def per_device(
    pair_rep,
    norm_gain,
    norm_bias,
    w_a_proj,
    w_a_gate,
    w_b_proj,
    w_b_gate,
    w_gate,
    out_gain,
    out_bias,
    w_out,
):
    hidden = w_a_proj.shape[1]
    w_inner = jnp.concatenate([w_a_proj, w_a_gate, w_b_proj, w_b_gate], axis=1)
    normed = layer_norm(pair_rep.astype(jnp.float32), norm_gain, norm_bias, -1).astype(jnp.bfloat16)
    inner = jnp.einsum("rkc,cm->mrk", normed, w_inner, preferred_element_type=jnp.float32)
    left_local = (jax.nn.sigmoid(inner[hidden : 2 * hidden]) * inner[:hidden]).astype(jnp.bfloat16)
    right_local = (
        jax.nn.sigmoid(inner[3 * hidden : 4 * hidden]) * inner[2 * hidden : 3 * hidden]
    ).astype(jnp.bfloat16)
    gating = jax.nn.sigmoid(
        jnp.einsum("rkc,cd->rkd", normed, w_gate, preferred_element_type=jnp.float32)
    ).astype(jnp.bfloat16)
    left_chan, right_chan = (
        lax.all_to_all(left_local, "row", split_axis=0, concat_axis=1, tiled=True),
        lax.all_to_all(right_local, "row", split_axis=0, concat_axis=1, tiled=True),
    )
    left_rows = lax.all_to_all(left_chan, "sub", split_axis=1, concat_axis=2, tiled=True)
    triangle = jnp.einsum(
        "hik,hjk->hij",
        left_rows,
        lax.all_gather(right_chan, "sub", axis=2, tiled=True),
        preferred_element_type=jnp.float32,
    ).astype(jnp.bfloat16)
    regrouped = lax.all_to_all(
        lax.all_to_all(triangle, "sub", split_axis=2, concat_axis=1, tiled=True),
        "row",
        split_axis=1,
        concat_axis=0,
        tiled=True,
    )
    hidden_normed = layer_norm(
        regrouped.astype(jnp.float32), out_gain[:, None, None], out_bias[:, None, None], 0
    ).astype(jnp.bfloat16)
    mixed = jnp.einsum("hrj,hc->rjc", hidden_normed, w_out, preferred_element_type=jnp.float32)
    return (gating.astype(jnp.float32) * mixed).astype(jnp.bfloat16)


def kernel(
    n_row,
    pair_hbm,
    ngain_hbm,
    nbias_hbm,
    wap_hbm,
    wag_hbm,
    wbp_hbm,
    wbg_hbm,
    wg_hbm,
    ogain_hbm,
    obias_hbm,
    wo_hbm,
    out_ref,
    pair_v,
    vec_v,
    w_v,
    wo_v,
    right_send,
    right_buf,
    left_buf,
    tri_v,
    in_sem,
    send_sem,
    recv_sem,
    left_sem,
    ready,
):
    rows, cols, chan = pair_v.shape
    hidden = right_send.shape[-1]
    half = n_row // 2
    row = lax.axis_index("row")
    sub = lax.axis_index("sub")
    other = 1 - sub
    owner = row // half
    slot = lax.rem(row, half)
    near = sub == owner
    low = owner == 0
    high_near = jnp.logical_and(near, jnp.logical_not(low))
    high_far = jnp.logical_not(jnp.logical_or(near, low))

    loads = [
        pltpu.make_async_copy(pair_hbm, pair_v, in_sem.at[0]),
        pltpu.make_async_copy(ngain_hbm, vec_v.at[0], in_sem.at[1]),
        pltpu.make_async_copy(nbias_hbm, vec_v.at[1], in_sem.at[2]),
        pltpu.make_async_copy(wbp_hbm, w_v.at[:, 0:hidden], in_sem.at[3]),
        pltpu.make_async_copy(wbg_hbm, w_v.at[:, hidden : 2 * hidden], in_sem.at[4]),
        pltpu.make_async_copy(wap_hbm, w_v.at[:, 2 * hidden : 3 * hidden], in_sem.at[5]),
        pltpu.make_async_copy(wag_hbm, w_v.at[:, 3 * hidden : 4 * hidden], in_sem.at[6]),
        pltpu.make_async_copy(wg_hbm, w_v.at[:, 4 * hidden : 4 * hidden + chan], in_sem.at[7]),
        pltpu.make_async_copy(ogain_hbm, vec_v.at[2], in_sem.at[8]),
        pltpu.make_async_copy(obias_hbm, vec_v.at[3], in_sem.at[9]),
        pltpu.make_async_copy(wo_hbm, wo_v, in_sem.at[10]),
    ]
    for load in loads:
        load.start()

    barrier = pltpu.get_barrier_semaphore()

    def greet(semaphore, target_row, target_sub):
        pl.semaphore_signal(
            semaphore,
            inc=1,
            device_id={"row": target_row, "sub": target_sub},
            device_id_type=pl.DeviceIdType.MESH,
        )

    @pl.when(low)
    def _():
        for step in range(half):
            greet(barrier, half + step, 0)

            @pl.when(sub == 1)
            def _():
                greet(barrier, half + step, 1)

    @pl.when(near)
    def _():
        for step in range(1, half):
            greet(barrier, owner * half + lax.rem(slot + step, half), owner)

    @pl.when(low)
    def _():
        greet(barrier, row, other)

        @pl.when(near)
        def _():
            for step in range(1, half):
                greet(barrier, lax.rem(slot + step, half), 1)

    @pl.when(high_far)
    def _():
        for step in range(half):
            greet(barrier, half + step, 1)
        pl.semaphore_wait(barrier, 2 * half)
        for step in range(half):
            for source_sub in range(2):
                greet(ready, step, source_sub)

    for load in loads[:3]:
        load.wait()
    pair = pair_v[...].astype(jnp.float32).reshape(rows * cols, chan)
    normed = layer_norm(pair, vec_v[0], vec_v[1], -1).astype(jnp.bfloat16)
    for load in loads[3:5]:
        load.wait()
    inner = jnp.dot(normed, w_v[:, 0 : 2 * hidden], preferred_element_type=jnp.float32)
    right = jax.nn.sigmoid(inner[:, hidden:]) * inner[:, :hidden]
    right = right.astype(jnp.bfloat16).reshape(rows, cols, hidden)
    right_send[...] = right

    @pl.when(owner == sub)
    def _():
        right_buf[slot, sub] = right

    @pl.when(low)
    def _():
        pl.semaphore_wait(barrier, half)

    @pl.when(high_near)
    def _():
        pl.semaphore_wait(barrier, 3 * half - 1)

    left_copy = pltpu.make_async_remote_copy(
        src_ref=left_buf.at[sub],
        dst_ref=left_buf.at[sub],
        send_sem=send_sem.at[n_row],
        recv_sem=left_sem,
        device_id={"sub": other},
        device_id_type=pl.DeviceIdType.MESH,
    )

    def right_copy(index, target):
        return pltpu.make_async_remote_copy(
            src_ref=right_send,
            dst_ref=right_buf.at[slot, sub],
            send_sem=send_sem.at[index],
            recv_sem=recv_sem.at[slot, sub],
            device_id={"row": target, "sub": owner},
            device_id_type=pl.DeviceIdType.MESH,
        )

    inside = [right_copy(q, owner * half + q) for q in range(half)]
    across = [right_copy(half + q, (1 - owner) * half + q) for q in range(half)]

    @pl.when(jnp.logical_not(low))
    def _():
        for copy in across:
            copy.start()

    @pl.when(high_near)
    def _():
        for step in range(half):
            greet(ready, half + step, 0)

    @pl.when(high_far)
    def _():
        pl.semaphore_wait(ready, half)

    for q in range(half):

        @pl.when(jnp.logical_not(jnp.logical_and(near, slot == q)))
        def _():
            inside[q].start()

    for load in loads[5:7]:
        load.wait()
    inner = jnp.dot(
        normed, w_v[:, 2 * hidden : 4 * hidden], preferred_element_type=jnp.float32
    )
    left = jax.nn.sigmoid(inner[:, hidden:]) * inner[:, :hidden]
    left_buf[sub] = left.astype(jnp.bfloat16).reshape(rows, cols, hidden)

    left_copy.start()

    @pl.when(low)
    def _():
        pl.semaphore_wait(ready, half)
        for copy in across[::-1]:
            copy.start()

    loads[7].wait()
    gating = jax.nn.sigmoid(
        jnp.dot(
            normed, w_v[:, 4 * hidden : 4 * hidden + chan], preferred_element_type=jnp.float32
        )
    ).astype(jnp.bfloat16)
    for load in loads[8:]:
        load.wait()

    left_copy.wait_recv()
    left_all = left_buf[...].astype(jnp.float32)
    for source in range(half):
        for source_sub in range(2):
            mine = jnp.logical_and(sub * half + source == row, sub == source_sub)

            @pl.when(jnp.logical_not(mine))
            def _():
                pltpu.make_async_remote_copy(
                    src_ref=right_send,
                    dst_ref=right_buf.at[source, source_sub],
                    send_sem=send_sem.at[0],
                    recv_sem=recv_sem.at[source, source_sub],
                    device_id={"sub": other},
                    device_id_type=pl.DeviceIdType.MESH,
                ).wait_recv()

        block = right_buf[source].astype(jnp.float32)
        for i in range(rows):
            prod = left_all[:, i][:, None] * block
            prod = prod[0] + prod[1]
            prod = jnp.sum(prod.reshape(rows, cols // 8, 8, hidden), axis=1)
            tri_v[i, source * rows : (source + 1) * rows, :] = jnp.sum(prod, axis=1)

    tri = tri_v[...].reshape(rows * cols, hidden).astype(jnp.bfloat16).astype(jnp.float32)
    hidden_normed = layer_norm(tri, vec_v[2], vec_v[3], -1).astype(jnp.bfloat16)
    mixed = jnp.dot(hidden_normed, wo_v[...], preferred_element_type=jnp.float32)
    out = (gating.astype(jnp.float32) * mixed).astype(jnp.bfloat16)
    out_ref[...] = out.reshape(rows, cols, chan)

    left_copy.wait_send()
    for q in range(half):

        @pl.when(jnp.logical_not(jnp.logical_and(near, slot == q)))
        def _():
            inside[q].wait_send()

        across[q].wait_send()


def one_round(n_row, pair_rep, norm_gain, norm_bias, *rest):
    w_a_proj, w_a_gate, w_b_proj, w_b_gate, w_gate, out_gain, out_bias, w_out = rest
    rows, cols, chan = pair_rep.shape
    hidden = w_a_proj.shape[1]
    half = n_row // 2
    hbm = pl.BlockSpec(memory_space=pltpu.HBM)
    return pl.pallas_call(
        functools.partial(kernel, n_row),
        out_shape=pltpu.VMEM((rows, cols, chan), jnp.bfloat16),
        in_specs=[hbm] * 11,
        out_specs=pl.BlockSpec(memory_space=pltpu.VMEM),
        scratch_shapes=[
            pltpu.VMEM((rows, cols, chan), jnp.bfloat16),
            pltpu.VMEM((4, 1, chan), jnp.float32),
            pltpu.VMEM((chan, 4 * hidden + chan), jnp.bfloat16),
            pltpu.VMEM((hidden, chan), jnp.bfloat16),
            pltpu.VMEM((rows, cols, hidden), jnp.bfloat16),
            pltpu.VMEM((half, 2, rows, cols, hidden), jnp.bfloat16),
            pltpu.VMEM((2, rows, cols, hidden), jnp.bfloat16),
            pltpu.VMEM((rows, cols, hidden), jnp.float32),
            pltpu.SemaphoreType.DMA((11,)),
            pltpu.SemaphoreType.DMA((n_row + 1,)),
            pltpu.SemaphoreType.DMA((half, 2)),
            pltpu.SemaphoreType.DMA,
            pltpu.SemaphoreType.REGULAR,
        ],
        compiler_params=pltpu.CompilerParams(
            collective_id=0, has_side_effects=True, vmem_limit_bytes=16 * 2**20
        ),
    )(
        *(
            pltpu.with_memory_space_constraint(operand, pltpu.HBM)
            for operand in (
                pair_rep,
                norm_gain.reshape(1, chan),
                norm_bias.reshape(1, chan),
                w_a_proj,
                w_a_gate,
                w_b_proj,
                w_b_gate,
                w_gate,
                out_gain.reshape(1, hidden),
                out_bias.reshape(1, hidden),
                w_out,
            )
        )
    )


def body(n_row, n_sub, *operands):
    rows, cols, _ = operands[0].shape
    hidden = operands[3].shape[1]
    gathered = cols * cols * n_sub * hidden * 2
    if n_sub == 2 and n_row % 2 == 0 and cols % 16 == 0 and gathered <= 4 * 2**20:
        return one_round(n_row, *operands)
    return per_device(*operands)


def solution(mesh):
    in_specs = (P(("grp", "row"), "sub", None), P(), P(), P(), P(), P(), P(), P(), P(), P(), P())
    out_specs = P(("grp", "row"), "sub", None)
    return jax.shard_map(
        functools.partial(body, mesh.shape["row"], mesh.shape["sub"]),
        mesh=mesh,
        in_specs=in_specs,
        out_specs=out_specs,
        check_vma=False,
    )
```

```python
import functools

import jax
import jax.numpy as jnp
from jax import lax
from jax.experimental import pallas as pl
from jax.experimental.pallas import tpu as pltpu
from jax.sharding import PartitionSpec as P

EPSILON = 1e-05


def layer_norm(values, gain, shift, axis):
    centred = values - jnp.mean(values, axis=axis, keepdims=True)
    variance = jnp.mean(centred * centred, axis=axis, keepdims=True)
    return centred * lax.rsqrt(variance + EPSILON) * gain + shift


def per_device(
    pair_rep,
    norm_gain,
    norm_bias,
    w_a_proj,
    w_a_gate,
    w_b_proj,
    w_b_gate,
    w_gate,
    out_gain,
    out_bias,
    w_out,
):
    hidden = w_a_proj.shape[1]
    w_inner = jnp.concatenate([w_a_proj, w_a_gate, w_b_proj, w_b_gate], axis=1)
    normed = layer_norm(pair_rep.astype(jnp.float32), norm_gain, norm_bias, -1).astype(jnp.bfloat16)
    inner = jnp.einsum("rkc,cm->mrk", normed, w_inner, preferred_element_type=jnp.float32)
    left_local = (jax.nn.sigmoid(inner[hidden : 2 * hidden]) * inner[:hidden]).astype(jnp.bfloat16)
    right_local = (
        jax.nn.sigmoid(inner[3 * hidden : 4 * hidden]) * inner[2 * hidden : 3 * hidden]
    ).astype(jnp.bfloat16)
    gating = jax.nn.sigmoid(
        jnp.einsum("rkc,cd->rkd", normed, w_gate, preferred_element_type=jnp.float32)
    ).astype(jnp.bfloat16)
    left_chan, right_chan = (
        lax.all_to_all(left_local, "row", split_axis=0, concat_axis=1, tiled=True),
        lax.all_to_all(right_local, "row", split_axis=0, concat_axis=1, tiled=True),
    )
    left_rows = lax.all_to_all(left_chan, "sub", split_axis=1, concat_axis=2, tiled=True)
    triangle = jnp.einsum(
        "hik,hjk->hij",
        left_rows,
        lax.all_gather(right_chan, "sub", axis=2, tiled=True),
        preferred_element_type=jnp.float32,
    ).astype(jnp.bfloat16)
    regrouped = lax.all_to_all(
        lax.all_to_all(triangle, "sub", split_axis=2, concat_axis=1, tiled=True),
        "row",
        split_axis=1,
        concat_axis=0,
        tiled=True,
    )
    hidden_normed = layer_norm(
        regrouped.astype(jnp.float32), out_gain[:, None, None], out_bias[:, None, None], 0
    ).astype(jnp.bfloat16)
    mixed = jnp.einsum("hrj,hc->rjc", hidden_normed, w_out, preferred_element_type=jnp.float32)
    return (gating.astype(jnp.float32) * mixed).astype(jnp.bfloat16)


def kernel(
    n_row,
    pair_hbm,
    ngain_hbm,
    nbias_hbm,
    wap_hbm,
    wag_hbm,
    wbp_hbm,
    wbg_hbm,
    wg_hbm,
    ogain_hbm,
    obias_hbm,
    wo_hbm,
    out_ref,
    pair_v,
    vec_v,
    w_v,
    wo_v,
    right_send,
    right_buf,
    left_buf,
    tri_v,
    in_sem,
    send_sem,
    recv_sem,
    left_sem,
    ready,
):
    rows, cols, chan = pair_v.shape
    hidden = right_send.shape[-1]
    half = n_row // 2
    row = lax.axis_index("row")
    sub = lax.axis_index("sub")
    other = 1 - sub
    owner = row // half
    slot = lax.rem(row, half)
    near = sub == owner
    low = owner == 0
    high_near = jnp.logical_and(near, jnp.logical_not(low))
    high_far = jnp.logical_not(jnp.logical_or(near, low))

    loads = [
        pltpu.make_async_copy(pair_hbm, pair_v, in_sem.at[0]),
        pltpu.make_async_copy(ngain_hbm, vec_v.at[0], in_sem.at[1]),
        pltpu.make_async_copy(nbias_hbm, vec_v.at[1], in_sem.at[2]),
        pltpu.make_async_copy(wbp_hbm, w_v.at[:, 0:hidden], in_sem.at[3]),
        pltpu.make_async_copy(wbg_hbm, w_v.at[:, hidden : 2 * hidden], in_sem.at[4]),
        pltpu.make_async_copy(wap_hbm, w_v.at[:, 2 * hidden : 3 * hidden], in_sem.at[5]),
        pltpu.make_async_copy(wag_hbm, w_v.at[:, 3 * hidden : 4 * hidden], in_sem.at[6]),
        pltpu.make_async_copy(wg_hbm, w_v.at[:, 4 * hidden : 4 * hidden + chan], in_sem.at[7]),
        pltpu.make_async_copy(ogain_hbm, vec_v.at[2], in_sem.at[8]),
        pltpu.make_async_copy(obias_hbm, vec_v.at[3], in_sem.at[9]),
        pltpu.make_async_copy(wo_hbm, wo_v, in_sem.at[10]),
    ]
    for load in loads:
        load.start()

    barrier = pltpu.get_barrier_semaphore()

    def greet(semaphore, target_row, target_sub):
        pl.semaphore_signal(
            semaphore,
            inc=1,
            device_id={"row": target_row, "sub": target_sub},
            device_id_type=pl.DeviceIdType.MESH,
        )

    @pl.when(low)
    def _():
        for step in range(half):
            greet(barrier, half + step, 0)

            @pl.when(sub == 1)
            def _():
                greet(barrier, half + step, 1)

    @pl.when(near)
    def _():
        for step in range(1, half):
            greet(barrier, owner * half + lax.rem(slot + step, half), owner)

    @pl.when(low)
    def _():
        greet(barrier, row, other)

        @pl.when(near)
        def _():
            for step in range(1, half):
                greet(barrier, lax.rem(slot + step, half), 1)

    @pl.when(high_far)
    def _():
        for step in range(half):
            greet(barrier, half + step, 1)
        pl.semaphore_wait(barrier, 2 * half)
        for step in range(half):
            for source_sub in range(2):
                greet(ready, step, source_sub)

    for load in loads[:3]:
        load.wait()
    pair = pair_v[...].astype(jnp.float32).reshape(rows * cols, chan)
    normed = layer_norm(pair, vec_v[0], vec_v[1], -1).astype(jnp.bfloat16)
    for load in loads[3:5]:
        load.wait()
    inner = jnp.dot(normed, w_v[:, 0 : 2 * hidden], preferred_element_type=jnp.float32)
    right = jax.nn.sigmoid(inner[:, hidden:]) * inner[:, :hidden]
    right = right.astype(jnp.bfloat16).reshape(rows, cols, hidden)
    right_send[...] = right

    @pl.when(owner == sub)
    def _():
        right_buf[slot, sub] = right

    @pl.when(low)
    def _():
        pl.semaphore_wait(barrier, half)

    @pl.when(high_near)
    def _():
        pl.semaphore_wait(barrier, 3 * half - 1)

    left_copy = pltpu.make_async_remote_copy(
        src_ref=left_buf.at[sub],
        dst_ref=left_buf.at[sub],
        send_sem=send_sem.at[n_row],
        recv_sem=left_sem,
        device_id={"sub": other},
        device_id_type=pl.DeviceIdType.MESH,
    )

    def right_copy(index, target):
        return pltpu.make_async_remote_copy(
            src_ref=right_send,
            dst_ref=right_buf.at[slot, sub],
            send_sem=send_sem.at[index],
            recv_sem=recv_sem.at[slot, sub],
            device_id={"row": target, "sub": owner},
            device_id_type=pl.DeviceIdType.MESH,
        )

    inside = [right_copy(q, owner * half + q) for q in range(half)]
    across = [right_copy(half + q, (1 - owner) * half + q) for q in range(half)]

    @pl.when(jnp.logical_not(low))
    def _():
        for copy in across:
            copy.start()

    @pl.when(high_near)
    def _():
        for step in range(half):
            greet(ready, half + step, 0)

    @pl.when(high_far)
    def _():
        pl.semaphore_wait(ready, half)

    for q in range(half):

        @pl.when(jnp.logical_not(jnp.logical_and(near, slot == q)))
        def _():
            inside[q].start()

    for load in loads[5:7]:
        load.wait()
    inner = jnp.dot(
        normed, w_v[:, 2 * hidden : 4 * hidden], preferred_element_type=jnp.float32
    )
    left = jax.nn.sigmoid(inner[:, hidden:]) * inner[:, :hidden]
    left_buf[sub] = left.astype(jnp.bfloat16).reshape(rows, cols, hidden)

    left_copy.start()

    @pl.when(low)
    def _():
        pl.semaphore_wait(ready, half)
        for copy in across[::2][::-1] + across[1::2][::-1]:
            copy.start()

    loads[7].wait()
    gating = jax.nn.sigmoid(
        jnp.dot(
            normed, w_v[:, 4 * hidden : 4 * hidden + chan], preferred_element_type=jnp.float32
        )
    ).astype(jnp.bfloat16)
    for load in loads[8:]:
        load.wait()

    left_copy.wait_recv()
    left_all = left_buf[...].astype(jnp.float32)
    for source in range(half):
        for source_sub in range(2):
            mine = jnp.logical_and(sub * half + source == row, sub == source_sub)

            @pl.when(jnp.logical_not(mine))
            def _():
                pltpu.make_async_remote_copy(
                    src_ref=right_send,
                    dst_ref=right_buf.at[source, source_sub],
                    send_sem=send_sem.at[0],
                    recv_sem=recv_sem.at[source, source_sub],
                    device_id={"sub": other},
                    device_id_type=pl.DeviceIdType.MESH,
                ).wait_recv()

        block = right_buf[source].astype(jnp.float32)
        for i in range(rows):
            prod = left_all[:, i][:, None] * block
            prod = prod[0] + prod[1]
            prod = jnp.sum(prod.reshape(rows, cols // 8, 8, hidden), axis=1)
            tri_v[i, source * rows : (source + 1) * rows, :] = jnp.sum(prod, axis=1)

    tri = tri_v[...].reshape(rows * cols, hidden).astype(jnp.bfloat16).astype(jnp.float32)
    hidden_normed = layer_norm(tri, vec_v[2], vec_v[3], -1).astype(jnp.bfloat16)
    mixed = jnp.dot(hidden_normed, wo_v[...], preferred_element_type=jnp.float32)
    out = (gating.astype(jnp.float32) * mixed).astype(jnp.bfloat16)
    out_ref[...] = out.reshape(rows, cols, chan)

    left_copy.wait_send()
    for q in range(half):

        @pl.when(jnp.logical_not(jnp.logical_and(near, slot == q)))
        def _():
            inside[q].wait_send()

        across[q].wait_send()


def one_round(n_row, pair_rep, norm_gain, norm_bias, *rest):
    w_a_proj, w_a_gate, w_b_proj, w_b_gate, w_gate, out_gain, out_bias, w_out = rest
    rows, cols, chan = pair_rep.shape
    hidden = w_a_proj.shape[1]
    half = n_row // 2
    hbm = pl.BlockSpec(memory_space=pltpu.HBM)
    return pl.pallas_call(
        functools.partial(kernel, n_row),
        out_shape=pltpu.VMEM((rows, cols, chan), jnp.bfloat16),
        in_specs=[hbm] * 11,
        out_specs=pl.BlockSpec(memory_space=pltpu.VMEM),
        scratch_shapes=[
            pltpu.VMEM((rows, cols, chan), jnp.bfloat16),
            pltpu.VMEM((4, 1, chan), jnp.float32),
            pltpu.VMEM((chan, 4 * hidden + chan), jnp.bfloat16),
            pltpu.VMEM((hidden, chan), jnp.bfloat16),
            pltpu.VMEM((rows, cols, hidden), jnp.bfloat16),
            pltpu.VMEM((half, 2, rows, cols, hidden), jnp.bfloat16),
            pltpu.VMEM((2, rows, cols, hidden), jnp.bfloat16),
            pltpu.VMEM((rows, cols, hidden), jnp.float32),
            pltpu.SemaphoreType.DMA((11,)),
            pltpu.SemaphoreType.DMA((n_row + 1,)),
            pltpu.SemaphoreType.DMA((half, 2)),
            pltpu.SemaphoreType.DMA,
            pltpu.SemaphoreType.REGULAR,
        ],
        compiler_params=pltpu.CompilerParams(
            collective_id=0, has_side_effects=True, vmem_limit_bytes=16 * 2**20
        ),
    )(
        *(
            pltpu.with_memory_space_constraint(operand, pltpu.HBM)
            for operand in (
                pair_rep,
                norm_gain.reshape(1, chan),
                norm_bias.reshape(1, chan),
                w_a_proj,
                w_a_gate,
                w_b_proj,
                w_b_gate,
                w_gate,
                out_gain.reshape(1, hidden),
                out_bias.reshape(1, hidden),
                w_out,
            )
        )
    )


def body(n_row, n_sub, *operands):
    rows, cols, _ = operands[0].shape
    hidden = operands[3].shape[1]
    gathered = cols * cols * n_sub * hidden * 2
    if n_sub == 2 and n_row % 2 == 0 and cols % 16 == 0 and gathered <= 4 * 2**20:
        return one_round(n_row, *operands)
    return per_device(*operands)


def solution(mesh):
    in_specs = (P(("grp", "row"), "sub", None), P(), P(), P(), P(), P(), P(), P(), P(), P(), P())
    out_specs = P(("grp", "row"), "sub", None)
    return jax.shard_map(
        functools.partial(body, mesh.shape["row"], mesh.shape["sub"]),
        mesh=mesh,
        in_specs=in_specs,
        out_specs=out_specs,
        check_vma=False,
    )
```
